256 devices in a mesh: grp: 32 (over z, y), ulys: 8 (over x, core).
Axes of the slice: x: 4, y: 4, z: 8, core: 2. Of those that a mesh axis runs over, the one named last changes fastest.
Arguments:
- layer_states: bfloat16 [32, 512, 7168], P('grp', None, 'ulys'), may hold values from -64 to 64
- new_states: bfloat16 [3, 32, 7168], P(None, 'grp', 'ulys'), may hold values from -64 to 64
- out_proj: bfloat16 [5120, 5120], P('ulys'), may hold values from -0.3125 to 0.3125
- gain: bfloat16 [5120], replicated, may hold values from 0.5 to 1.5
- lengths: int32 [32], P('grp'), may hold values from 64 to 512, as said below
- finished: int32 [32], P('grp'), may hold values from 0 to 1, as said below
- assignment: int32 [32], replicated, may hold values from 0 to 31, as said below
Outputs:
- decoded: bfloat16 [3, 32, 5120], P(None, 'grp', 'ulys')
- scored: bfloat16 [32, 512, 5120], P('grp', 'ulys')
The draws below stay inside these ranges and needn't reach their ends.
Inputs may be any that keep to these rules, and one draw needn't show every extreme that they name: `lengths`: one row of each draw has length 512. Some row is finished and some row is not. `assignment`: for each r below 1, the entries r, 1 + r, 2 + r, ... form a permutation of the trainer groups.
All inputs are finite; a program needn't handle non-finite values.
Results may differ from the reference program's by a relative error of at most 0.019.
Values may be sent and summed in bfloat16 or wider, within the bound.
A program may use at most 64 MiB of HBM per device.

```python
import jax
import jax.numpy as jnp
from jax import lax

D = 5120
KH = 8
HD = 128
STEPS = 3
ROWS_G = 1
CACHE = 512
QPK = 5
GW = 896
ROWS = 32
N_GRP = 32


def draw_layer_states(key, part):
    key = jax.random.fold_in(key, 5)
    shape = (ROWS, CACHE, KH, QPK + 2, HD)
    full = jnp.clip(jax.random.normal(key, shape, jnp.float32), -5.0, 5.0)
    return full.reshape(ROWS, CACHE, KH * GW).astype(jnp.bfloat16)


def draw_new_states(key, part):
    key = jax.random.fold_in(key, 9)
    shape = (STEPS, ROWS, KH, QPK + 2, HD)
    full = jnp.clip(jax.random.normal(key, shape, jnp.float32), -5.0, 5.0)
    return full.reshape(STEPS, ROWS, KH * GW).astype(jnp.bfloat16)


def draw_lengths(key, part):
    key = jax.random.fold_in(key, 13)
    draw_key, pick_key = jax.random.split(key)
    values = jax.random.randint(draw_key, (ROWS,), CACHE // 8, CACHE + 1)
    chosen = jax.random.randint(pick_key, (), 0, ROWS)
    return jnp.where(jnp.arange(ROWS) == chosen, CACHE, values).astype(jnp.int32)


def draw_finished(key, part):
    key = jax.random.fold_in(key, 21)
    flag_key, open_key, done_key = jax.random.split(key, 3)
    flags = jax.random.randint(flag_key, (ROWS,), 0, 2)
    open_row = jax.random.randint(open_key, (), 0, ROWS)
    done_row = (open_row + 1 + jax.random.randint(done_key, (), 0, ROWS - 1)) % ROWS
    places = jnp.arange(ROWS)
    flags = jnp.where(places == open_row, 0, flags)
    flags = jnp.where(places == done_row, 1, flags)
    return flags.astype(jnp.int32)


def one_permutation(key):
    return jax.random.permutation(key, N_GRP)


def draw_assignment(key, part):
    key = jax.random.fold_in(key, 17)
    perms = jax.vmap(one_permutation)(jax.random.split(key, ROWS_G))
    return perms.T.reshape(ROWS).astype(jnp.int32)


def block_scale(key, extent, cuts, least, high):
    factor_of = 1.0
    for axis_at, parts in cuts:
        steps = jax.random.uniform(jax.random.fold_in(jax.random.fold_in(key, 6), axis_at), (parts,), jnp.float32, least / len(cuts), high / len(cuts))
        factor_of = factor_of * jnp.repeat(jnp.exp(steps), extent[axis_at] // parts).reshape((-1,) + (1,) * (len(extent) - 1 - axis_at))
    return factor_of


def normal_values(key, dims, width, most, cuts=(), kind=jnp.bfloat16):
    entries = width * jax.random.normal(key, dims, jnp.float32)
    if cuts:
        entries = entries * block_scale(key, dims, cuts, -0.22, 0.18)
    return jnp.clip(entries, -most, most).astype(kind)


def setup_inputs(seed: int = 0) -> dict:
    splits = jax.random.split(jax.random.key(seed), 8)
    layer_states = draw_layer_states(jax.random.fold_in(splits[7], 71), 0)
    new_states = draw_new_states(jax.random.fold_in(splits[7], 71), 0)
    out_proj = normal_values(splits[2], (D, D), (D // 16) ** -0.5, 0.3125, ((0, 8),))
    gain = jnp.clip(1.0 + 0.1 * jax.random.normal(splits[3], (D,), jnp.float32), 0.5, 1.5).astype(jnp.bfloat16)
    lengths = draw_lengths(jax.random.fold_in(splits[7], 71), 0)
    finished = draw_finished(jax.random.fold_in(splits[7], 71), 0)
    assignment = draw_assignment(jax.random.fold_in(splits[7], 71), 0)
    return {"layer_states": layer_states, "new_states": new_states, "out_proj": out_proj, "gain": gain, "lengths": lengths, "finished": finished, "assignment": assignment}


def masked_softmax(scores, mask):
    scores = jnp.where(mask, scores, -jnp.inf)
    top = lax.optimization_barrier(jnp.max(scores, axis=-1, keepdims=True))
    lifted = jnp.exp(scores - top)
    return (lifted / lax.optimization_barrier(jnp.sum(lifted, axis=-1, keepdims=True))).astype(jnp.bfloat16)

def decode_all(layer_states, new_states, out_proj, lengths, finished):
    shaped = layer_states.reshape(ROWS, CACHE, KH, QPK + 2, HD).astype(jnp.float32)
    keys = shaped[:, :, :, QPK, :]
    values = shaped[:, :, :, QPK + 1, :]
    fresh = new_states.reshape(STEPS, ROWS, KH, QPK + 2, HD).astype(jnp.float32)
    queries = fresh[:, :, :, :QPK, :]
    new_keys = fresh[:, :, :, QPK, :]
    new_values = fresh[:, :, :, QPK + 1, :]
    scale = HD ** (-0.5)
    old = jnp.einsum('srgqd,rjgd->srgqj', queries, keys) * scale
    recent = jnp.einsum('srgqd,trgd->srgqt', queries, new_keys) * scale
    old_mask = jnp.arange(CACHE, dtype=jnp.int32)[None, :] < lengths[:, None]
    old_mask = jnp.broadcast_to(old_mask[None, :, None, None, :], old.shape)
    order = jnp.arange(STEPS, dtype=jnp.int32)
    new_mask = order[None, :] <= order[:, None]
    new_mask = jnp.broadcast_to(new_mask[:, None, None, None, :], recent.shape)
    weights = masked_softmax(jnp.concatenate([old, recent], axis=-1), jnp.concatenate([old_mask, new_mask], axis=-1))
    weights = weights.astype(jnp.float32)
    heads = jnp.einsum('srgqj,rjgd->srgqd', weights[..., :CACHE], values)
    heads = heads + jnp.einsum('srgqt,trgd->srgqd', weights[..., CACHE:], new_values)
    heads = heads.astype(jnp.bfloat16).reshape(STEPS * ROWS, D)
    product = jnp.dot(heads, out_proj, preferred_element_type=jnp.float32).reshape(STEPS, ROWS, D)
    alive = (1 - finished).astype(jnp.float32)
    return (product * alive[None, :, None]).astype(jnp.bfloat16)

def attend_row(states, length, done, gain):
    shaped = states.reshape(CACHE, KH, QPK + 2, HD).astype(jnp.float32)
    queries = shaped[:, :, :QPK, :]
    keys = shaped[:, :, QPK, :]
    values = shaped[:, :, QPK + 1, :]
    block = min(512, CACHE)
    key_places = jnp.arange(CACHE, dtype=jnp.int32)
    pieces = []
    for start in range(0, CACHE, block):
        rows = queries[start:start + block]
        scores = jnp.einsum('igqd,jgd->gqij', rows, keys) * HD ** (-0.5)
        row_places = start + jnp.arange(block, dtype=jnp.int32)
        mask = (key_places[None, :] <= row_places[:, None]) & (key_places[None, :] < length)
        weights = masked_softmax(scores, mask[None, None]).astype(jnp.float32)
        out = jnp.einsum('gqij,jgd->igqd', weights, values)
        live = ((row_places < length) & (done > 0)).astype(jnp.float32)
        pieces.append((out * live[:, None, None, None]).astype(jnp.bfloat16).reshape(block, D))
    heads = jnp.concatenate(pieces, axis=0)
    lifted = heads.astype(jnp.float32)
    power = lax.optimization_barrier(jnp.mean(lifted * lifted, axis=-1, keepdims=True))
    return (lifted * lax.rsqrt(power + 1e-06) * gain.astype(jnp.float32)).astype(jnp.bfloat16)

def reference(layer_states, new_states, out_proj, gain, lengths, finished, assignment):
    decoded = decode_all(layer_states, new_states, out_proj, lengths, finished)

    def one_row(args):
        states, length, done = args
        return attend_row(states, length, done, gain)
    rows_out = lax.map(one_row, (layer_states, lengths, finished))
    dest = assignment * ROWS_G + jnp.arange(ROWS, dtype=jnp.int32) % ROWS_G
    scored = jnp.zeros((ROWS, CACHE, D), jnp.bfloat16).at[dest].set(rows_out)
    return (decoded, scored)
```

```python
import functools
import math

import jax
import jax.numpy as jnp
from jax import lax
from jax.experimental import pallas as pl
from jax.experimental.pallas import tpu as pltpu
from jax.sharding import PartitionSpec as P

HD = 128
QPK = 5
GW = 896
FEAT = QPK * HD
CACHE = 512
D = 5120
STEPS = 3
N_GRP = 32
N_ULYS = 8
N_Z = 8
N_Y = 4
PBLK = CACHE // N_ULYS
TILE = PBLK // N_Y
QBLK = 128
PAD = 8
WCHUNK = 1280
N_W = D // WCHUNK
EXP2_SCALE = HD ** (-0.5) * math.log2(math.e)
NEG = -1e30
MIB = 1024 * 1024


def attend(states, heads, length):
    rows = lax.broadcasted_iota(jnp.int32, (QBLK, 1), 0)
    cols = lax.broadcasted_iota(jnp.int32, (1, QBLK), 1)
    for b in range(CACHE // QBLK):
        top = b * QBLK
        span = top + QBLK
        keys = states[0:span, FEAT:FEAT + HD]
        values = states[0:span, FEAT + HD:FEAT + 2 * HD]
        live = rows + top < length
        for q in range(QPK):
            query = states[top:span, q * HD:(q + 1) * HD]
            s = lax.dot_general(query, keys, (((1,), (1,)), ((), ())), preferred_element_type=jnp.float32)
            diag = jnp.where(cols <= rows, s[:, top:span], NEG)
            s = diag if b == 0 else jnp.concatenate([s[:, :top], diag], axis=1)
            m = jnp.max(s, axis=1, keepdims=True)
            p = jnp.exp2((s - m) * EXP2_SCALE)
            total = jnp.sum(p, axis=1, keepdims=True)
            o = jnp.dot(p.astype(jnp.bfloat16), values, preferred_element_type=jnp.float32)
            o = jnp.where(live, o * (1.0 / total), 0.0)
            heads[top:span, q * HD:(q + 1) * HD] = o.astype(jnp.bfloat16)


def decode_heads(states, fresh, dhead, length):
    keys = states[:, FEAT:FEAT + HD]
    values = states[:, FEAT + HD:FEAT + 2 * HD]
    new_keys = fresh[:, FEAT:FEAT + HD].astype(jnp.bfloat16)
    new_values = fresh[:, FEAT + HD:FEAT + 2 * HD].astype(jnp.bfloat16)
    old_mask = lax.broadcasted_iota(jnp.int32, (1, CACHE), 1) < length
    step = lax.broadcasted_iota(jnp.int32, (PAD, PAD), 0)
    new_mask = lax.broadcasted_iota(jnp.int32, (PAD, PAD), 1) <= step
    for q in range(QPK):
        query = fresh[:, q * HD:(q + 1) * HD].astype(jnp.bfloat16)
        dims = (((1,), (1,)), ((), ()))
        old = lax.dot_general(query, keys, dims, preferred_element_type=jnp.float32)
        new = lax.dot_general(query, new_keys, dims, preferred_element_type=jnp.float32)
        old = jnp.where(old_mask, old, NEG)
        new = jnp.where(new_mask, new, NEG)
        m = jnp.maximum(jnp.max(old, axis=1, keepdims=True), jnp.max(new, axis=1, keepdims=True))
        p_old = jnp.exp2((old - m) * EXP2_SCALE)
        p_new = jnp.exp2((new - m) * EXP2_SCALE)
        total = jnp.sum(p_old, axis=1, keepdims=True) + jnp.sum(p_new, axis=1, keepdims=True)
        o = jnp.dot(p_old.astype(jnp.bfloat16), values, preferred_element_type=jnp.float32)
        o = o + jnp.dot(p_new.astype(jnp.bfloat16), new_values, preferred_element_type=jnp.float32)
        dhead[:, q * HD:(q + 1) * HD] = (o * (1.0 / total)).astype(jnp.bfloat16)


def local_kernel(length_ref, done_ref, assign_ref, states, new, w_hbm, heads, part, source, fresh, dhead, w, w_sem):
    length = length_ref[0]
    done = done_ref[0]

    def w_copy(c):
        cols = pl.ds(c * WCHUNK, WCHUNK)
        return pltpu.make_async_copy(w_hbm.at[:, cols], w.at[c], w_sem.at[c])

    @pl.loop(0, N_GRP)
    def _(n):
        source[assign_ref[n]] = n

    @pl.when(done > 0)
    def _():
        part[...] = jnp.zeros_like(part)
        attend(states.at[0], heads, length)

    @pl.when(done <= 0)
    def _():
        for c in range(N_W):
            w_copy(c).start()
        heads[...] = jnp.zeros_like(heads)
        fresh[...] = jnp.zeros_like(fresh)
        for s in range(STEPS):
            fresh[s:s + 1, :] = new[s].astype(jnp.float32)
        decode_heads(states.at[0], fresh, dhead, length)
        lhs = dhead[...]
        for c in range(N_W):
            w_copy(c).wait()
            part[:, c * WCHUNK:(c + 1) * WCHUNK] = jnp.dot(lhs, w[c], preferred_element_type=jnp.float32)


def ring_kernel(source, heads, part, out, dec, recv, stage, dec_in, send1, recv1, send2, recv2, send3, recv3):
    me = lax.axis_index("grp")
    u = lax.axis_index("ulys")
    z = me // N_Y
    y = me % N_Y
    head_in = (z - u + N_Z) % N_Z
    has_self = jnp.where((head_in == u), 1, 0)

    barrier = pltpu.get_barrier_semaphore()

    @pl.loop(0, N_GRP)
    def _(n):
        @pl.when(jnp.logical_not((n == me) & (head_in == u)))
        def _():
            pl.semaphore_signal(barrier, inc=1, device_id=(n, head_in), device_id_type=pl.DeviceIdType.MESH)

        @pl.when(n != me)
        def _():
            pl.semaphore_signal(barrier, inc=1, device_id=(n, u), device_id_type=pl.DeviceIdType.MESH)

    @pl.loop(1, N_ULYS)
    def _(k):
        pl.semaphore_signal(barrier, inc=1, device_id=(me, (u + k) % N_ULYS), device_id_type=pl.DeviceIdType.MESH)

    own_hit = jnp.where(z == (2 * u) % N_Z, 1, 0)
    pl.semaphore_wait(barrier, N_GRP - own_hit + N_GRP - 1 + N_ULYS - 1)

    @pl.loop(0, N_GRP)
    def _(k):
        p = (k // N_Y + z) % N_ULYS
        r = (k + y) % N_Y
        target = ((u + p) % N_Z) * N_Y + r
        src = heads.at[pl.ds(pl.multiple_of(p * PBLK + r * TILE, TILE), TILE)]
        own = (target == me) & (p == u)

        @pl.when(own)
        def _():
            pltpu.make_async_copy(src, recv.at[me], recv1).start()

        @pl.when(jnp.logical_not(own))
        def _():
            pltpu.make_async_remote_copy(
                src, recv.at[me], send1, recv1, device_id=(target, p), device_id_type=pl.DeviceIdType.MESH
            ).start()

    @pl.loop(1, N_ULYS)
    def _(k):
        p = (u + k) % N_ULYS
        pltpu.make_async_remote_copy(
            part.at[:, pl.ds(pl.multiple_of(p * FEAT, HD), FEAT)],
            dec_in.at[u], send3, recv3, device_id=(me, p), device_id_type=pl.DeviceIdType.MESH
        ).start()

    pltpu.make_async_copy(part.at[:, pl.ds(pl.multiple_of(u * FEAT, HD), FEAT)], dec_in.at[u], recv3).start()
    pltpu.make_async_copy(dec_in, dec_in, recv3).wait()
    total = dec_in[0]
    for g in range(1, N_ULYS):
        total = total + dec_in[g]
    dec[...] = total

    pltpu.make_async_copy(recv, recv, recv1).wait()

    rows = pl.ds(pl.multiple_of(y * TILE, TILE), TILE)
    cols = pl.ds(pl.multiple_of(head_in * FEAT, HD), FEAT)

    @pl.loop(1, N_GRP)
    def _(k):
        t = (me + k) % N_GRP
        stage[t] = recv[source[t]]
        pltpu.make_async_remote_copy(
            stage.at[t], out.at[rows, cols], send2, recv2, device_id=(t, u), device_id_type=pl.DeviceIdType.MESH
        ).start()

    stage[me] = recv[source[me]]
    pltpu.make_async_copy(stage.at[me], out.at[rows, cols], recv2).start()

    @pl.when(own_hit > 0)
    def _():
        part_of = heads.at[pl.ds(0, CACHE - TILE)]
        pltpu.make_async_copy(part_of, part_of, send1).wait()

    @pl.when(own_hit <= 0)
    def _():
        pltpu.make_async_copy(heads, heads, send1).wait()

    sent = dec_in.at[pl.ds(0, N_ULYS - 1)]
    pltpu.make_async_copy(sent, sent, send3).wait()
    sent = stage.at[pl.ds(0, N_GRP - 1)]
    pltpu.make_async_copy(sent, sent, send2).wait()
    pltpu.make_async_copy(out, out, recv2).wait()


def norm_kernel(raw, dec, done_ref, gain, scored, decoded):
    @pl.when(pl.program_id(0) == 0)
    def _():
        alive = (1 - done_ref[0]).astype(jnp.float32)
        for s in range(STEPS):
            decoded[s] = (dec[s:s + 1, :] * alive).astype(jnp.bfloat16)

    lifted = raw[...].astype(jnp.float32)
    power = jnp.mean(lifted * lifted, axis=-1, keepdims=True)
    scored[0] = (lifted * lax.rsqrt(power + 1e-06) * gain[...].astype(jnp.float32)).astype(jnp.bfloat16)


def smem():
    return pl.BlockSpec(memory_space=pltpu.SMEM)


def vmem():
    return pl.BlockSpec(memory_space=pltpu.VMEM)


def hbm():
    return pl.BlockSpec(memory_space=pl.ANY)


def body(layer_states, new_states, out_proj, gain, lengths, finished, assignment):
    heads, part, source = pl.pallas_call(
        local_kernel,
        out_shape=(
            jax.ShapeDtypeStruct((CACHE, FEAT), jnp.bfloat16),
            jax.ShapeDtypeStruct((PAD, D), jnp.float32),
            jax.ShapeDtypeStruct((N_GRP,), jnp.int32),
        ),
        in_specs=[smem(), smem(), smem(), vmem(), vmem(), hbm()],
        out_specs=(vmem(), vmem(), smem()),
        scratch_shapes=[
            pltpu.VMEM((PAD, GW), jnp.float32),
            pltpu.VMEM((PAD, FEAT), jnp.bfloat16),
            pltpu.VMEM((N_W, FEAT, WCHUNK), jnp.bfloat16),
            pltpu.SemaphoreType.DMA((N_W,)),
        ],
        compiler_params=pltpu.CompilerParams(vmem_limit_bytes=32 * MIB),
        name="local",
    )(lengths, finished, assignment, layer_states, new_states, out_proj)
    raw, dec = pl.pallas_call(
        ring_kernel,
        out_shape=(
            jax.ShapeDtypeStruct((PBLK, D), jnp.bfloat16),
            jax.ShapeDtypeStruct((PAD, FEAT), jnp.float32),
        ),
        in_specs=[smem(), hbm(), hbm()],
        out_specs=(hbm(), vmem()),
        scratch_shapes=[
            pltpu.VMEM((N_GRP, TILE, FEAT), jnp.bfloat16),
            pltpu.VMEM((N_GRP, TILE, FEAT), jnp.bfloat16),
            pltpu.VMEM((N_ULYS, PAD, FEAT), jnp.float32),
        ] + [pltpu.SemaphoreType.DMA] * 6,
        compiler_params=pltpu.CompilerParams(
            vmem_limit_bytes=16 * MIB, collective_id=0, has_side_effects=True
        ),
        name="spread",
    )(source, heads, part)
    scored, decoded = pl.pallas_call(
        norm_kernel,
        grid=(N_Y,),
        out_shape=(
            jax.ShapeDtypeStruct((1, PBLK, D), jnp.bfloat16),
            jax.ShapeDtypeStruct((STEPS, 1, FEAT), jnp.bfloat16),
        ),
        in_specs=[
            pl.BlockSpec((TILE, D), lambda i: (i, 0)),
            pl.BlockSpec((PAD, FEAT), lambda i: (0, 0)),
            smem(),
            pl.BlockSpec((1, D), lambda i: (0, 0)),
        ],
        out_specs=(
            pl.BlockSpec((1, TILE, D), lambda i: (0, i, 0)),
            pl.BlockSpec((STEPS, 1, FEAT), lambda i: (0, 0, 0)),
        ),
        compiler_params=pltpu.CompilerParams(vmem_limit_bytes=16 * MIB),
        name="norm",
    )(raw, dec, finished, gain.reshape(1, D))
    return (decoded, scored)


def solution(mesh):
    placed = (
        P("grp", None, "ulys"),
        P(None, "grp", "ulys"),
        P("ulys", None),
        P(),
        P("grp"),
        P("grp"),
        P(),
    )
    return jax.shard_map(
        body,
        mesh=mesh,
        in_specs=placed,
        out_specs=(P(None, "grp", "ulys"), P("grp", "ulys", None)),
        check_vma=False,
    )
```

```python
import math

import jax
import jax.numpy as jnp
from jax import lax
from jax.experimental import pallas as pl
from jax.experimental.pallas import tpu as pltpu
from jax.sharding import PartitionSpec as P

HD = 128
QPK = 5
GW = 896
FEAT = QPK * HD
CACHE = 512
D = 5120
STEPS = 3
N_GRP = 32
N_ULYS = 8
N_Z = 8
N_Y = 4
PBLK = CACHE // N_ULYS
TILE = PBLK // N_Y
QBLK = 128
N_B = CACHE // QBLK
B_TILES = QBLK // TILE
PAD = 8
WCHUNK = 1280
N_W = D // WCHUNK
EXP2_SCALE = HD ** (-0.5) * math.log2(math.e)
NEG = -1e30
MIB = 1024 * 1024
MESH = pl.DeviceIdType.MESH
CHUNKS = (2, 3)
FIRST = tuple(sum(CHUNKS[:c]) for c in range(len(CHUNKS)))
N_C = len(CHUNKS)


def attend_block(x, out, b, first, count, limit):
    rows = lax.broadcasted_iota(jnp.int32, (QBLK, 1), 0)
    cols = lax.broadcasted_iota(jnp.int32, (1, QBLK), 1)
    top = b * QBLK
    span = top + QBLK
    keys = x[0:span, FEAT:FEAT + HD]
    values = x[0:span, FEAT + HD:FEAT + 2 * HD]
    live = rows + top < limit
    for j in range(count):
        q = first + j
        query = x[top:span, q * HD:(q + 1) * HD]
        s = lax.dot_general(query, keys, (((1,), (1,)), ((), ())), preferred_element_type=jnp.float32)
        diag = jnp.where(cols <= rows, s[:, top:span], NEG)
        s = diag if b == 0 else jnp.concatenate([s[:, :top], diag], axis=1)
        m = jnp.max(s, axis=1, keepdims=True)
        p = jnp.exp2((s - m) * EXP2_SCALE)
        total = jnp.sum(p, axis=1, keepdims=True)
        o = jnp.dot(p.astype(jnp.bfloat16), values, preferred_element_type=jnp.float32)
        o = jnp.where(live, o * (1.0 / total), 0.0)
        out[top:span, j * HD:(j + 1) * HD] = o.astype(jnp.bfloat16)


def decode_heads(x, fresh, dhead, length):
    keys = x[:, FEAT:FEAT + HD]
    values = x[:, FEAT + HD:FEAT + 2 * HD]
    new_keys = fresh[:, FEAT:FEAT + HD].astype(jnp.bfloat16)
    new_values = fresh[:, FEAT + HD:FEAT + 2 * HD].astype(jnp.bfloat16)
    old_mask = lax.broadcasted_iota(jnp.int32, (1, CACHE), 1) < length
    step = lax.broadcasted_iota(jnp.int32, (PAD, PAD), 0)
    new_mask = lax.broadcasted_iota(jnp.int32, (PAD, PAD), 1) <= step
    dims = (((1,), (1,)), ((), ()))
    for q in range(QPK):
        query = fresh[:, q * HD:(q + 1) * HD].astype(jnp.bfloat16)
        old = lax.dot_general(query, keys, dims, preferred_element_type=jnp.float32)
        new = lax.dot_general(query, new_keys, dims, preferred_element_type=jnp.float32)
        old = jnp.where(old_mask, old, NEG)
        new = jnp.where(new_mask, new, NEG)
        m = jnp.maximum(jnp.max(old, axis=1, keepdims=True), jnp.max(new, axis=1, keepdims=True))
        p_old = jnp.exp2((old - m) * EXP2_SCALE)
        p_new = jnp.exp2((new - m) * EXP2_SCALE)
        total = jnp.sum(p_old, axis=1, keepdims=True) + jnp.sum(p_new, axis=1, keepdims=True)
        o = jnp.dot(p_old.astype(jnp.bfloat16), values, preferred_element_type=jnp.float32)
        o = o + jnp.dot(p_new.astype(jnp.bfloat16), new_values, preferred_element_type=jnp.float32)
        dhead[:, q * HD:(q + 1) * HD] = (o * (1.0 / total)).astype(jnp.bfloat16)


def kernel(x_hbm, new_hbm, w_hbm, gain_hbm, length_s, done_s, assign_hbm, dec, scored, *scratch):
    heads, recv, stage = scratch[:N_C], scratch[N_C:2 * N_C], scratch[2 * N_C:3 * N_C]
    (raw, x, new, w, gain, assign, source, fresh, dhead, part, dec_in,
     x_sem, w_sem, small_sem, send1, recv1, send2, recv2, send3, recv3) = scratch[3 * N_C:]
    me = lax.axis_index("grp")
    u = lax.axis_index("ulys")
    z = me // N_Y
    y = me % N_Y
    i_in = (u - z + N_Z) % N_Z
    g_in = (2 * z - u + N_Z) % N_Z
    b_in = (y - i_in + 2 * N_Y) % N_Y
    p_out = 2 * b_in + i_in // N_Y
    r_out = i_in % N_Y
    hit1 = jnp.where(g_in == u, 1, 0)
    hit2 = jnp.where(p_out == u, 1, 0)

    small = [
        pltpu.make_async_copy(src, dst, small_sem.at[k])
        for k, (src, dst) in enumerate(
            ((assign_hbm, assign), (new_hbm, new), (gain_hbm, gain)))
    ]
    x_copies = [
        pltpu.make_async_copy(x_hbm.at[0, pl.ds(b * QBLK, QBLK)], x.at[pl.ds(b * QBLK, QBLK)], x_sem.at[b])
        for b in range(N_B)
    ]
    w_copies = [
        pltpu.make_async_copy(w_hbm.at[:, pl.ds(c * WCHUNK, WCHUNK)], w.at[c], w_sem.at[c]) for c in range(N_W)
    ]
    for copy in x_copies[:1] + small + x_copies[1:] + w_copies:
        copy.start()

    barrier = pltpu.get_barrier_semaphore()

    def greet(grp, ulys):
        pl.semaphore_signal(barrier, inc=1, device_id=(grp, ulys), device_id_type=MESH)

    @pl.loop(0, N_GRP)
    def _(n):
        @pl.when(jnp.logical_not((n == me) & (g_in == u)))
        def _():
            greet(n, g_in)

        g = n // N_Y
        i = N_Y * (u % 2) + n % N_Y
        grp = ((g + i) % N_Z) * N_Y + (u // 2 + i) % N_Y
        ulys = (g + 2 * i) % N_ULYS

        @pl.when(jnp.logical_not((grp == me) & (ulys == u)))
        def _():
            greet(grp, ulys)

    @pl.loop(1, N_ULYS)
    def _(k):
        greet(me, (u + k) % N_ULYS)

    length = length_s[0]
    done = done_s[0]
    limit = length * done

    for c in range(N_C):
        for b in range(N_B):
            if c == 0:
                x_copies[b].wait()
            attend_block(x, heads[c], b, FIRST[c], CHUNKS[c], limit)
            if c == 0 and b == 0:
                pl.semaphore_wait(barrier, 2 * N_GRP - hit1 - hit2 + N_ULYS - 1)

            @pl.loop(0, B_TILES)
            def _(k, c=c, b=b):
                i = (k + y + z) % B_TILES
                grp = ((u + i) % N_Z) * N_Y + (b + i) % N_Y
                ulys = (u + 2 * i) % N_ULYS
                src = heads[c].at[pl.ds(pl.multiple_of(b * QBLK + i * TILE, TILE), TILE)]
                own = (grp == me) & (ulys == u)

                @pl.when(own)
                def _():
                    pltpu.make_async_copy(src, recv[c].at[me], recv1.at[c]).start()

                @pl.when(jnp.logical_not(own))
                def _():
                    pltpu.make_async_remote_copy(
                        src, recv[c].at[me], send1.at[c], recv1.at[c], device_id=(grp, ulys), device_id_type=MESH
                    ).start()

    small[0].wait()

    @pl.loop(0, N_GRP)
    def _(t):
        found = 0
        for n in range(N_GRP):
            found = jnp.where(assign[n] == t, n, found)
        source[t] = found

    small[1].wait()
    fresh[...] = jnp.zeros_like(fresh)
    fresh[0:STEPS, :] = new[...].astype(jnp.float32)
    decode_heads(x, fresh, dhead, length)
    lhs = dhead[...]
    for c in range(N_W):
        w_copies[c].wait()
        part[:, c * WCHUNK:(c + 1) * WCHUNK] = jnp.dot(lhs, w[c], preferred_element_type=jnp.float32)

    @pl.loop(1, N_ULYS)
    def _(k):
        p = (u + k) % N_ULYS
        pltpu.make_async_remote_copy(
            part.at[:, pl.ds(pl.multiple_of(p * FEAT, HD), FEAT)],
            dec_in.at[u], send3, recv3, device_id=(me, p), device_id_type=MESH
        ).start()

    pltpu.make_async_copy(part.at[:, pl.ds(pl.multiple_of(u * FEAT, HD), FEAT)], dec_in.at[u], recv3).start()

    rows = pl.ds(pl.multiple_of(r_out * TILE, TILE), TILE)
    for c in range(N_C):
        width = CHUNKS[c] * HD
        cols = pl.ds(pl.multiple_of(g_in * FEAT + FIRST[c] * HD, HD), width)
        pltpu.make_async_copy(recv[c], recv[c], recv1.at[c]).wait()

        @pl.loop(0, N_GRP)
        def _(k, c=c, cols=cols):
            t = (me + k) % N_GRP
            stage[c][t] = recv[c][source[t]]
            own = (t == me) & (p_out == u)

            @pl.when(own)
            def _():
                pltpu.make_async_copy(stage[c].at[t], raw.at[rows, cols], recv2.at[c]).start()

            @pl.when(jnp.logical_not(own))
            def _():
                pltpu.make_async_remote_copy(
                    stage[c].at[t], raw.at[rows, cols], send2.at[c], recv2.at[c],
                    device_id=(t, p_out), device_id_type=MESH
                ).start()

    pltpu.make_async_copy(dec_in, dec_in, recv3).wait()
    total = dec_in[0]
    for g in range(1, N_ULYS):
        total = total + dec_in[g]
    dec[...] = (total * (1 - done).astype(jnp.float32))[0:STEPS].astype(jnp.bfloat16)

    small[2].wait()
    square = jnp.zeros((PBLK, HD), jnp.float32)
    for c in range(N_C):
        pltpu.make_async_copy(recv[c], recv[c], recv2.at[c]).wait()
        for g in range(N_ULYS):
            for q in range(FIRST[c], FIRST[c] + CHUNKS[c]):
                at = (g * QPK + q) * HD
                part_of = raw[:, at:at + HD].astype(jnp.float32)
                square = square + part_of * part_of
    power = jnp.sum(square, axis=1, keepdims=True) * (1.0 / D)
    factor = lax.rsqrt(power + 1e-06)
    gains = gain[...].astype(jnp.float32)
    for k in range(D // HD):
        lifted = raw[:, k * HD:(k + 1) * HD].astype(jnp.float32)
        scored[:, k * HD:(k + 1) * HD] = (lifted * factor * gains[k:k + 1]).astype(jnp.bfloat16)

    for sems, hit in ((send1, hit1), (send2, hit2)):
        for c in range(N_C):
            @pl.when(hit > 0)
            def _(c=c, sems=sems):
                sent = stage[c].at[pl.ds(0, N_GRP - 1)]
                pltpu.make_async_copy(sent, sent, sems.at[c]).wait()

            @pl.when(hit <= 0)
            def _(c=c, sems=sems):
                pltpu.make_async_copy(stage[c], stage[c], sems.at[c]).wait()
    sent = dec_in.at[pl.ds(0, N_ULYS - 1)]
    pltpu.make_async_copy(sent, sent, send3).wait()


def body(layer_states, new_states, out_proj, gain, lengths, finished, assignment):
    hbm = pl.BlockSpec(memory_space=pltpu.HBM)
    smem = pl.BlockSpec(memory_space=pltpu.SMEM)
    vmem = pl.BlockSpec(memory_space=pltpu.VMEM)
    dec, scored = pl.pallas_call(
        kernel,
        out_shape=(
            jax.ShapeDtypeStruct((STEPS, FEAT), jnp.bfloat16),
            jax.ShapeDtypeStruct((PBLK, D), jnp.bfloat16),
        ),
        in_specs=[hbm] * 4 + [smem] * 2 + [hbm],
        out_specs=(vmem, vmem),
        scratch_shapes=[pltpu.VMEM((CACHE, n * HD), jnp.bfloat16) for n in CHUNKS]
        + [pltpu.VMEM((N_GRP, TILE, n * HD), jnp.bfloat16) for n in CHUNKS] * 2
        + [
            pltpu.VMEM((PBLK, D), jnp.bfloat16),
            pltpu.VMEM((CACHE, GW), jnp.bfloat16),
            pltpu.VMEM((STEPS, GW), jnp.bfloat16),
            pltpu.VMEM((N_W, FEAT, WCHUNK), jnp.bfloat16),
            pltpu.VMEM((D // HD, HD), jnp.bfloat16),
            pltpu.SMEM((N_GRP,), jnp.int32),
            pltpu.SMEM((N_GRP,), jnp.int32),
            pltpu.VMEM((PAD, GW), jnp.float32),
            pltpu.VMEM((PAD, FEAT), jnp.bfloat16),
            pltpu.VMEM((PAD, D), jnp.float32),
            pltpu.VMEM((N_ULYS, PAD, FEAT), jnp.float32),
            pltpu.SemaphoreType.DMA((N_B,)),
            pltpu.SemaphoreType.DMA((N_W,)),
            pltpu.SemaphoreType.DMA((3,)),
        ]
        + [pltpu.SemaphoreType.DMA((N_C,))] * 4
        + [pltpu.SemaphoreType.DMA] * 2,
        compiler_params=pltpu.CompilerParams(
            vmem_limit_bytes=56 * MIB, collective_id=0, has_side_effects=True
        ),
        name="step",
    )(layer_states, new_states.reshape(STEPS, GW), out_proj, gain.reshape(D // HD, HD), lengths, finished, assignment)
    return (dec.reshape(STEPS, 1, FEAT), scored.reshape(1, PBLK, D))


def solution(mesh):
    placed = (
        P("grp", None, "ulys"),
        P(None, "grp", "ulys"),
        P("ulys", None),
        P(),
        P("grp"),
        P("grp"),
        P(),
    )
    return jax.shard_map(
        body,
        mesh=mesh,
        in_specs=placed,
        out_specs=(P(None, "grp", "ulys"), P("grp", "ulys", None)),
        check_vma=False,
    )
```

```python
import math

import jax
import jax.numpy as jnp
from jax import lax
from jax.experimental import pallas as pl
from jax.experimental.pallas import tpu as pltpu
from jax.sharding import PartitionSpec as P

HD = 128
QPK = 5
GW = 896
FEAT = QPK * HD
CACHE = 512
D = 5120
STEPS = 3
N_GRP = 32
N_ULYS = 8
N_Z = 8
N_Y = 4
PBLK = CACHE // N_ULYS
TILE = PBLK // N_Y
QBLK = 128
N_B = CACHE // QBLK
B_TILES = QBLK // TILE
PAD = 8
WCHUNK = 1280
N_W = D // WCHUNK
EXP2_SCALE = HD ** (-0.5) * math.log2(math.e)
NEG = -1e30
MIB = 1024 * 1024
MESH = pl.DeviceIdType.MESH
CHUNKS = (2, 3)
OUT = pltpu.VMEM
VLIM = 32
FIRST = tuple(sum(CHUNKS[:c]) for c in range(len(CHUNKS)))
N_C = len(CHUNKS)


def relay_of(head, b, i):
    p = 2 * b + i // N_Y
    return ((head + p) % N_Z) * N_Y + (b + i) % N_Y, p


def tile_of(z, y, u):
    b = u // 2
    r = (y - b + N_Y) % N_Y
    return (z - u + N_Z) % N_Z, b, (u % 2) * N_Y + r


def attend_block(x, out, b, first, count, limit):
    rows = lax.broadcasted_iota(jnp.int32, (QBLK, 1), 0)
    cols = lax.broadcasted_iota(jnp.int32, (1, QBLK), 1)
    top = b * QBLK
    span = top + QBLK
    keys = x[0:span, FEAT:FEAT + HD]
    values = x[0:span, FEAT + HD:FEAT + 2 * HD]
    live = rows + top < limit
    for j in range(count):
        q = first + j
        query = x[top:span, q * HD:(q + 1) * HD]
        s = lax.dot_general(query, keys, (((1,), (1,)), ((), ())), preferred_element_type=jnp.float32)
        diag = jnp.where(cols <= rows, s[:, top:span], NEG)
        s = diag if b == 0 else jnp.concatenate([s[:, :top], diag], axis=1)
        m = jnp.max(s, axis=1, keepdims=True)
        p = jnp.exp2((s - m) * EXP2_SCALE)
        total = jnp.sum(p, axis=1, keepdims=True)
        o = jnp.dot(p.astype(jnp.bfloat16), values, preferred_element_type=jnp.float32)
        o = jnp.where(live, o * (1.0 / total), 0.0)
        out[top:span, j * HD:(j + 1) * HD] = o.astype(jnp.bfloat16)


def decode_heads(x, fresh, dhead, length):
    keys = x[:, FEAT:FEAT + HD]
    values = x[:, FEAT + HD:FEAT + 2 * HD]
    new_keys = fresh[:, FEAT:FEAT + HD].astype(jnp.bfloat16)
    new_values = fresh[:, FEAT + HD:FEAT + 2 * HD].astype(jnp.bfloat16)
    old_mask = lax.broadcasted_iota(jnp.int32, (1, CACHE), 1) < length
    step = lax.broadcasted_iota(jnp.int32, (PAD, PAD), 0)
    new_mask = lax.broadcasted_iota(jnp.int32, (PAD, PAD), 1) <= step
    dims = (((1,), (1,)), ((), ()))
    for q in range(QPK):
        query = fresh[:, q * HD:(q + 1) * HD].astype(jnp.bfloat16)
        old = lax.dot_general(query, keys, dims, preferred_element_type=jnp.float32)
        new = lax.dot_general(query, new_keys, dims, preferred_element_type=jnp.float32)
        old = jnp.where(old_mask, old, NEG)
        new = jnp.where(new_mask, new, NEG)
        m = jnp.maximum(jnp.max(old, axis=1, keepdims=True), jnp.max(new, axis=1, keepdims=True))
        p_old = jnp.exp2((old - m) * EXP2_SCALE)
        p_new = jnp.exp2((new - m) * EXP2_SCALE)
        total = jnp.sum(p_old, axis=1, keepdims=True) + jnp.sum(p_new, axis=1, keepdims=True)
        o = jnp.dot(p_old.astype(jnp.bfloat16), values, preferred_element_type=jnp.float32)
        o = o + jnp.dot(p_new.astype(jnp.bfloat16), new_values, preferred_element_type=jnp.float32)
        dhead[:, q * HD:(q + 1) * HD] = (o * (1.0 / total)).astype(jnp.bfloat16)


def step_kernel(x_hbm, new_hbm, w_hbm, length_s, done_s, assign_hbm, dec, raw, *scratch):
    heads, recv, stage = scratch[:N_C], scratch[N_C:2 * N_C], scratch[2 * N_C:3 * N_C]
    (x, new, w, assign, found, source, fresh, dhead, part, dec_in,
     x_sem, w_sem, small_sem, send1, recv1, send2, recv2, send3, recv3) = scratch[3 * N_C:]
    me = lax.axis_index("grp")
    u = lax.axis_index("ulys")
    z = me // N_Y
    y = me % N_Y
    g_in, b_in, i_in = tile_of(z, y, u)
    p_out = 2 * b_in + i_in // N_Y
    r_out = i_in % N_Y
    hit1 = jnp.where(g_in == u, 1, 0)
    hit2 = jnp.where(p_out == u, 1, 0)

    small = [
        pltpu.make_async_copy(src, dst, small_sem.at[k])
        for k, (src, dst) in enumerate(
            ((assign_hbm, assign), (new_hbm, new)))
    ]
    x_copies = [
        pltpu.make_async_copy(x_hbm.at[0, pl.ds(b * QBLK, QBLK)], x.at[pl.ds(b * QBLK, QBLK)], x_sem.at[b])
        for b in range(N_B)
    ]
    w_copies = [
        pltpu.make_async_copy(w_hbm.at[:, pl.ds(c * WCHUNK, WCHUNK)], w.at[c], w_sem.at[c]) for c in range(N_W)
    ]
    for copy in x_copies[:1] + small + x_copies[1:] + w_copies:
        copy.start()

    barrier = pltpu.get_barrier_semaphore()

    def greet(grp, ulys):
        pl.semaphore_signal(barrier, inc=1, device_id=(grp, ulys), device_id_type=MESH)

    @pl.loop(0, N_GRP, unroll=8)
    def _(n):
        @pl.when(jnp.logical_not((n == me) & (g_in == u)))
        def _():
            greet(n, g_in)

        grp, ulys = relay_of(n // N_Y, u // 2, N_Y * (u % 2) + n % N_Y)

        @pl.when(jnp.logical_not((grp == me) & (ulys == u)))
        def _():
            greet(grp, ulys)

    @pl.loop(1, N_ULYS)
    def _(k):
        greet(me, (u + k) % N_ULYS)

    length = length_s[0]
    done = done_s[0]
    limit = length * done

    for c in range(N_C):
        for b in range(N_B):
            if c == 0:
                x_copies[b].wait()
            attend_block(x, heads[c], b, FIRST[c], CHUNKS[c], limit)
        if c == 0:
            pl.semaphore_wait(barrier, 2 * N_GRP - hit1 - hit2 + N_ULYS - 1)

        @pl.loop(0, N_GRP)
        def _(k, c=c):
            b = (k // B_TILES + z + y) % N_B
            i = (k + y + z) % B_TILES
            grp, ulys = relay_of(u, b, i)
            src = heads[c].at[pl.ds(pl.multiple_of(b * QBLK + i * TILE, TILE), TILE)]
            own = (grp == me) & (ulys == u)

            @pl.when(own)
            def _():
                pltpu.make_async_copy(src, recv[c].at[me], recv1.at[c]).start()

            @pl.when(jnp.logical_not(own))
            def _():
                pltpu.make_async_remote_copy(
                    src, recv[c].at[me], send1.at[c], recv1.at[c], device_id=(grp, ulys), device_id_type=MESH
                ).start()

    small[0].wait()
    place = lax.broadcasted_iota(jnp.int32, (N_GRP, HD), 0)
    group = jnp.zeros((N_GRP, HD), jnp.int32)
    for n in range(N_GRP):
        group = jnp.where(place == n, assign[n], group)
    lanes = lax.broadcasted_iota(jnp.int32, (N_GRP, HD), 1)
    found[...] = jnp.max(jnp.where(group == lanes, place, 0), axis=0, keepdims=True)
    to_scalars = pltpu.make_async_copy(found, source, small_sem.at[0])
    to_scalars.start()
    to_scalars.wait()

    rows = pl.ds(pl.multiple_of(r_out * TILE, TILE), TILE)
    for c in range(N_C):
        width = CHUNKS[c] * HD
        cols = pl.ds(pl.multiple_of(g_in * FEAT + FIRST[c] * HD, HD), width)
        pltpu.make_async_copy(recv[c], recv[c], recv1.at[c]).wait()

        @pl.loop(0, N_GRP)
        def _(k, c=c, cols=cols):
            t = (k // 4) * N_Y + (k + y) % N_Y
            stage[c][t] = recv[c][source[0, t]]
            own = (t == me) & (p_out == u)

            @pl.when(own)
            def _():
                pltpu.make_async_copy(stage[c].at[t], raw.at[rows, cols], recv2.at[c]).start()

            @pl.when(jnp.logical_not(own))
            def _():
                pltpu.make_async_remote_copy(
                    stage[c].at[t], raw.at[rows, cols], send2.at[c], recv2.at[c],
                    device_id=(t, p_out), device_id_type=MESH
                ).start()

        if c > 0:
            continue
        small[1].wait()
        fresh[...] = jnp.zeros_like(fresh)
        fresh[0:STEPS, :] = new[...].astype(jnp.float32)
        decode_heads(x, fresh, dhead, length)
        lhs = dhead[...]
        for k in range(N_W):
            w_copies[k].wait()
            part[:, k * WCHUNK:(k + 1) * WCHUNK] = jnp.dot(lhs, w[k], preferred_element_type=jnp.float32)

        @pl.loop(1, N_ULYS)
        def _(k):
            p = (u + k) % N_ULYS
            pltpu.make_async_remote_copy(
                part.at[:, pl.ds(pl.multiple_of(p * FEAT, HD), FEAT)],
                dec_in.at[u], send3, recv3, device_id=(me, p), device_id_type=MESH
            ).start()

        pltpu.make_async_copy(part.at[:, pl.ds(pl.multiple_of(u * FEAT, HD), FEAT)], dec_in.at[u], recv3).start()

    pltpu.make_async_copy(dec_in, dec_in, recv3).wait()
    total = dec_in[0]
    for g in range(1, N_ULYS):
        total = total + dec_in[g]
    dec[...] = (total * (1 - done).astype(jnp.float32))[0:STEPS].astype(jnp.bfloat16)

    for c in range(N_C):
        pltpu.make_async_copy(recv[c], recv[c], recv2.at[c]).wait()
    for sems, hit in ((send1, hit1), (send2, hit2)):
        for c in range(N_C):
            @pl.when(hit > 0)
            def _(c=c, sems=sems):
                sent = stage[c].at[pl.ds(0, N_GRP - 1)]
                pltpu.make_async_copy(sent, sent, sems.at[c]).wait()

            @pl.when(hit <= 0)
            def _(c=c, sems=sems):
                pltpu.make_async_copy(stage[c], stage[c], sems.at[c]).wait()
    sent = dec_in.at[pl.ds(0, N_ULYS - 1)]
    pltpu.make_async_copy(sent, sent, send3).wait()


def norm_kernel(raw, dec, gain, decoded, scored, out, sem):
    decoded[...] = dec[...]
    gains = gain[...].astype(jnp.float32)
    copies = []
    for r in range(N_Y):
        rows = slice(r * TILE, (r + 1) * TILE)
        square = jnp.zeros((TILE, HD), jnp.float32)
        for k in range(D // HD):
            lifted = raw[rows, k * HD:(k + 1) * HD].astype(jnp.float32)
            square = square + lifted * lifted
        power = jnp.sum(square, axis=1, keepdims=True) * (1.0 / D)
        factor = lax.rsqrt(power + 1e-06)
        for k in range(D // HD):
            lifted = raw[rows, k * HD:(k + 1) * HD].astype(jnp.float32)
            out[rows, k * HD:(k + 1) * HD] = (lifted * factor * gains[k:k + 1]).astype(jnp.bfloat16)
        at = pl.ds(r * TILE, TILE)
        copies.append(pltpu.make_async_copy(out.at[at], scored.at[at], sem.at[r]))
        copies[-1].start()
    for copy in copies:
        copy.wait()


def body(layer_states, new_states, out_proj, gain, lengths, finished, assignment):
    hbm = pl.BlockSpec(memory_space=pl.ANY)
    vmem = pl.BlockSpec(memory_space=pltpu.VMEM)
    smem = pl.BlockSpec(memory_space=pltpu.SMEM)

    def pinned(a):
        return pltpu.with_memory_space_constraint(a, pltpu.HBM)

    dec, raw = pl.pallas_call(
        step_kernel,
        out_shape=(
            OUT((STEPS, FEAT), jnp.bfloat16),
            OUT((PBLK, D), jnp.bfloat16),
        ),
        in_specs=[hbm] * 3 + [smem] * 2 + [hbm],
        out_specs=(vmem, vmem),
        scratch_shapes=[pltpu.VMEM((CACHE, n * HD), jnp.bfloat16) for n in CHUNKS]
        + [pltpu.VMEM((N_GRP, TILE, n * HD), jnp.bfloat16) for n in CHUNKS] * 2
        + [
            pltpu.VMEM((CACHE, GW), jnp.bfloat16),
            pltpu.VMEM((STEPS, GW), jnp.bfloat16),
            pltpu.VMEM((N_W, FEAT, WCHUNK), jnp.bfloat16),
            pltpu.SMEM((N_GRP,), jnp.int32),
            pltpu.VMEM((1, HD), jnp.int32),
            pltpu.SMEM((1, HD), jnp.int32),
            pltpu.VMEM((PAD, GW), jnp.float32),
            pltpu.VMEM((PAD, FEAT), jnp.bfloat16),
            pltpu.VMEM((PAD, D), jnp.float32),
            pltpu.VMEM((N_ULYS, PAD, FEAT), jnp.float32),
            pltpu.SemaphoreType.DMA((N_B,)),
            pltpu.SemaphoreType.DMA((N_W,)),
            pltpu.SemaphoreType.DMA((2,)),
        ]
        + [pltpu.SemaphoreType.DMA((N_C,))] * 4
        + [pltpu.SemaphoreType.DMA] * 2,
        compiler_params=pltpu.CompilerParams(
            vmem_limit_bytes=VLIM * MIB, collective_id=0, has_side_effects=True
        ),
        name="step",
    )(
        pinned(layer_states), pinned(new_states.reshape(STEPS, GW)), pinned(out_proj),
        lengths, finished, pinned(assignment),
    )
    decoded, scored = pl.pallas_call(
        norm_kernel,
        out_shape=(
            jax.ShapeDtypeStruct((STEPS, FEAT), jnp.bfloat16),
            jax.ShapeDtypeStruct((PBLK, D), jnp.bfloat16),
        ),
        in_specs=[vmem] * 3,
        out_specs=(vmem, hbm),
        scratch_shapes=[pltpu.VMEM((PBLK, D), jnp.bfloat16), pltpu.SemaphoreType.DMA((N_Y,))],
        compiler_params=pltpu.CompilerParams(vmem_limit_bytes=8 * MIB),
        name="norm",
    )(raw, dec, gain.reshape(D // HD, HD))
    return (decoded.reshape(STEPS, 1, FEAT), scored.reshape(1, PBLK, D))


def solution(mesh):
    placed = (
        P("grp", None, "ulys"),
        P(None, "grp", "ulys"),
        P("ulys", None),
        P(),
        P("grp"),
        P("grp"),
        P(),
    )
    return jax.shard_map(
        body,
        mesh=mesh,
        in_specs=placed,
        out_specs=(P(None, "grp", "ulys"), P("grp", "ulys", None)),
        check_vma=False,
    )
```

```python
import math

import jax
import jax.numpy as jnp
from jax import lax
from jax.experimental import pallas as pl
from jax.experimental.pallas import tpu as pltpu
from jax.sharding import PartitionSpec as P

HD = 128
QPK = 5
GW = 896
FEAT = QPK * HD
CACHE = 512
D = 5120
STEPS = 3
N_GRP = 32
N_ULYS = 8
N_Z = 8
N_Y = 4
PBLK = CACHE // N_ULYS
TILE = PBLK // N_Y
QBLK = 128
N_B = CACHE // QBLK
B_TILES = QBLK // TILE
PAD = 8
WCHUNK = 1280
N_W = D // WCHUNK
EXP2_SCALE = HD ** (-0.5) * math.log2(math.e)
NEG = -1e30
MIB = 1024 * 1024
MESH = pl.DeviceIdType.MESH
CHUNKS = (2, 3)

VLIM = 32
FIRST = tuple(sum(CHUNKS[:c]) for c in range(len(CHUNKS)))
N_C = len(CHUNKS)


def relay_of(head, b, i):
    p = 2 * b + i // N_Y
    return ((head + p) % N_Z) * N_Y + (b + i) % N_Y, p


def tile_of(z, y, u):
    b = u // 2
    r = (y - b + N_Y) % N_Y
    return (z - u + N_Z) % N_Z, b, (u % 2) * N_Y + r


def attend_block(x, out, b, first, count, limit):
    rows = lax.broadcasted_iota(jnp.int32, (QBLK, 1), 0)
    cols = lax.broadcasted_iota(jnp.int32, (1, QBLK), 1)
    top = b * QBLK
    span = top + QBLK
    keys = x[0:span, FEAT:FEAT + HD]
    values = x[0:span, FEAT + HD:FEAT + 2 * HD]
    live = rows + top < limit
    for j in range(count):
        q = first + j
        query = x[top:span, q * HD:(q + 1) * HD]
        s = lax.dot_general(query, keys, (((1,), (1,)), ((), ())), preferred_element_type=jnp.float32)
        diag = jnp.where(cols <= rows, s[:, top:span], NEG)
        s = diag if b == 0 else jnp.concatenate([s[:, :top], diag], axis=1)
        m = jnp.max(s, axis=1, keepdims=True)
        p = jnp.exp2((s - m) * EXP2_SCALE)
        total = jnp.sum(p, axis=1, keepdims=True)
        o = jnp.dot(p.astype(jnp.bfloat16), values, preferred_element_type=jnp.float32)
        o = jnp.where(live, o * (1.0 / total), 0.0)
        out[top:span, j * HD:(j + 1) * HD] = o.astype(jnp.bfloat16)


def decode_heads(x, fresh, dhead, length):
    keys = x[:, FEAT:FEAT + HD]
    values = x[:, FEAT + HD:FEAT + 2 * HD]
    new_keys = fresh[:, FEAT:FEAT + HD].astype(jnp.bfloat16)
    new_values = fresh[:, FEAT + HD:FEAT + 2 * HD].astype(jnp.bfloat16)
    old_mask = lax.broadcasted_iota(jnp.int32, (1, CACHE), 1) < length
    step = lax.broadcasted_iota(jnp.int32, (PAD, PAD), 0)
    new_mask = lax.broadcasted_iota(jnp.int32, (PAD, PAD), 1) <= step
    dims = (((1,), (1,)), ((), ()))
    for q in range(QPK):
        query = fresh[:, q * HD:(q + 1) * HD].astype(jnp.bfloat16)
        old = lax.dot_general(query, keys, dims, preferred_element_type=jnp.float32)
        new = lax.dot_general(query, new_keys, dims, preferred_element_type=jnp.float32)
        old = jnp.where(old_mask, old, NEG)
        new = jnp.where(new_mask, new, NEG)
        m = jnp.maximum(jnp.max(old, axis=1, keepdims=True), jnp.max(new, axis=1, keepdims=True))
        p_old = jnp.exp2((old - m) * EXP2_SCALE)
        p_new = jnp.exp2((new - m) * EXP2_SCALE)
        total = jnp.sum(p_old, axis=1, keepdims=True) + jnp.sum(p_new, axis=1, keepdims=True)
        o = jnp.dot(p_old.astype(jnp.bfloat16), values, preferred_element_type=jnp.float32)
        o = o + jnp.dot(p_new.astype(jnp.bfloat16), new_values, preferred_element_type=jnp.float32)
        dhead[:, q * HD:(q + 1) * HD] = (o * (1.0 / total)).astype(jnp.bfloat16)


def step_kernel(x_hbm, new_hbm, w_hbm, length_s, done_s, assign_hbm, dec, raw, *scratch):
    heads, recv, stage = scratch[:N_C], scratch[N_C:2 * N_C], scratch[2 * N_C:3 * N_C]
    (x, new, w, assign, found, source, fresh, dhead, part, dec_in,
     x_sem, w_sem, small_sem, send1, recv1, send2, recv2, send3, recv3) = scratch[3 * N_C:]
    me = lax.axis_index("grp")
    u = lax.axis_index("ulys")
    z = me // N_Y
    y = me % N_Y
    g_in, b_in, i_in = tile_of(z, y, u)
    p_out = 2 * b_in + i_in // N_Y
    r_out = i_in % N_Y
    hit1 = jnp.where(g_in == u, 1, 0)
    hit2 = jnp.where(p_out == u, 1, 0)

    small = [
        pltpu.make_async_copy(src, dst, small_sem.at[k])
        for k, (src, dst) in enumerate(
            ((assign_hbm, assign), (new_hbm, new)))
    ]
    x_copies = [
        pltpu.make_async_copy(x_hbm.at[0, pl.ds(b * QBLK, QBLK)], x.at[pl.ds(b * QBLK, QBLK)], x_sem.at[b])
        for b in range(N_B)
    ]
    w_copies = [
        pltpu.make_async_copy(w_hbm.at[:, pl.ds(c * WCHUNK, WCHUNK)], w.at[c], w_sem.at[c]) for c in range(N_W)
    ]
    for copy in x_copies[:1] + small + x_copies[1:] + w_copies:
        copy.start()

    barrier = pltpu.get_barrier_semaphore()

    def greet(grp, ulys):
        pl.semaphore_signal(barrier, inc=1, device_id=(grp, ulys), device_id_type=MESH)

    @pl.loop(0, N_GRP, unroll=8)
    def _(n):
        @pl.when(jnp.logical_not((n == me) & (g_in == u)))
        def _():
            greet(n, g_in)

    @pl.loop(1, N_ULYS)
    def _(k):
        greet(me, (u + k) % N_ULYS)

    length = length_s[0]
    done = done_s[0]
    limit = length * done

    for c in range(N_C):
        for b in range(N_B):
            if c == 0:
                x_copies[b].wait()
            attend_block(x, heads[c], b, FIRST[c], CHUNKS[c], limit)
        if c == 0:
            pl.semaphore_wait(barrier, N_GRP - hit1 + N_ULYS - 1)

        @pl.loop(0, N_GRP)
        def _(k, c=c):
            b = (k // B_TILES + z + y) % N_B
            i = (k + y + z) % B_TILES
            grp, ulys = relay_of(u, b, i)
            src = heads[c].at[pl.ds(pl.multiple_of(b * QBLK + i * TILE, TILE), TILE)]
            own = (grp == me) & (ulys == u)

            @pl.when(own)
            def _():
                pltpu.make_async_copy(src, recv[c].at[me], recv1.at[c]).start()

            @pl.when(jnp.logical_not(own))
            def _():
                pltpu.make_async_remote_copy(
                    src, recv[c].at[me], send1.at[c], recv1.at[c], device_id=(grp, ulys), device_id_type=MESH
                ).start()

    small[0].wait()
    place = lax.broadcasted_iota(jnp.int32, (N_GRP, HD), 0)
    group = jnp.zeros((N_GRP, HD), jnp.int32)
    for n in range(N_GRP):
        group = jnp.where(place == n, assign[n], group)
    lanes = lax.broadcasted_iota(jnp.int32, (N_GRP, HD), 1)
    found[...] = jnp.max(jnp.where(group == lanes, place, 0), axis=0, keepdims=True)
    to_scalars = pltpu.make_async_copy(found, source, small_sem.at[0])
    to_scalars.start()
    to_scalars.wait()

    rows = pl.ds(pl.multiple_of(r_out * TILE, TILE), TILE)
    for c in range(N_C):
        width = CHUNKS[c] * HD
        cols = pl.ds(pl.multiple_of(g_in * FEAT + FIRST[c] * HD, HD), width)
        pltpu.make_async_copy(recv[c], recv[c], recv1.at[c]).wait()

        @pl.loop(0, N_GRP)
        def _(k, c=c, cols=cols):
            t = k
            stage[c][t] = recv[c][source[0, t]]
            own = (t == me) & (p_out == u)

            @pl.when(own)
            def _():
                pltpu.make_async_copy(stage[c].at[t], raw.at[rows, cols], recv2.at[c]).start()

            @pl.when(jnp.logical_not(own))
            def _():
                pltpu.make_async_remote_copy(
                    stage[c].at[t], raw.at[rows, cols], send2.at[c], recv2.at[c],
                    device_id=(t, p_out), device_id_type=MESH
                ).start()

        if c > 0:
            continue
        small[1].wait()
        fresh[...] = jnp.zeros_like(fresh)
        fresh[0:STEPS, :] = new[...].astype(jnp.float32)
        decode_heads(x, fresh, dhead, length)
        lhs = dhead[...]
        for k in range(N_W):
            w_copies[k].wait()
            part[:, k * WCHUNK:(k + 1) * WCHUNK] = jnp.dot(lhs, w[k], preferred_element_type=jnp.float32)

        @pl.loop(1, N_ULYS)
        def _(k):
            p = (u + k) % N_ULYS
            pltpu.make_async_remote_copy(
                part.at[:, pl.ds(pl.multiple_of(p * FEAT, HD), FEAT)],
                dec_in.at[u], send3, recv3, device_id=(me, p), device_id_type=MESH
            ).start()

        pltpu.make_async_copy(part.at[:, pl.ds(pl.multiple_of(u * FEAT, HD), FEAT)], dec_in.at[u], recv3).start()

    pltpu.make_async_copy(dec_in, dec_in, recv3).wait()
    total = dec_in[0]
    for g in range(1, N_ULYS):
        total = total + dec_in[g]
    dec[...] = (total * (1 - done).astype(jnp.float32))[0:STEPS].astype(jnp.bfloat16)

    for c in range(N_C):
        pltpu.make_async_copy(recv[c], recv[c], recv2.at[c]).wait()
    for sems, hit in ((send1, hit1), (send2, hit2)):
        for c in range(N_C):
            @pl.when(hit > 0)
            def _(c=c, sems=sems):
                sent = stage[c].at[pl.ds(0, N_GRP - 1)]
                pltpu.make_async_copy(sent, sent, sems.at[c]).wait()

            @pl.when(hit <= 0)
            def _(c=c, sems=sems):
                pltpu.make_async_copy(stage[c], stage[c], sems.at[c]).wait()
    sent = dec_in.at[pl.ds(0, N_ULYS - 1)]
    pltpu.make_async_copy(sent, sent, send3).wait()


def norm_kernel(raw, dec, gain, decoded, scored, out, sem):
    copies = [pltpu.make_async_copy(dec, decoded, sem.at[N_Y])]
    copies[0].start()
    gains = gain[...].astype(jnp.float32)
    for r in range(N_Y):
        rows = slice(r * TILE, (r + 1) * TILE)
        square = jnp.zeros((TILE, HD), jnp.float32)
        for k in range(D // HD):
            lifted = raw[rows, k * HD:(k + 1) * HD].astype(jnp.float32)
            square = square + lifted * lifted
        power = jnp.sum(square, axis=1, keepdims=True) * (1.0 / D)
        factor = lax.rsqrt(power + 1e-06)
        for k in range(D // HD):
            lifted = raw[rows, k * HD:(k + 1) * HD].astype(jnp.float32)
            out[rows, k * HD:(k + 1) * HD] = (lifted * factor * gains[k:k + 1]).astype(jnp.bfloat16)
        at = pl.ds(r * TILE, TILE)
        copies.append(pltpu.make_async_copy(out.at[at], scored.at[at], sem.at[r]))
        copies[-1].start()
    for copy in copies:
        copy.wait()


def body(layer_states, new_states, out_proj, gain, lengths, finished, assignment):
    hbm = pl.BlockSpec(memory_space=pl.ANY)
    vmem = pl.BlockSpec(memory_space=pltpu.VMEM)
    smem = pl.BlockSpec(memory_space=pltpu.SMEM)

    def pinned(a):
        return pltpu.with_memory_space_constraint(a, pltpu.HBM)

    dec, raw = pl.pallas_call(
        step_kernel,
        out_shape=(
            pltpu.VMEM((STEPS, FEAT), jnp.bfloat16),
            pltpu.VMEM((PBLK, D), jnp.bfloat16),
        ),
        in_specs=[hbm] * 3 + [smem] * 2 + [hbm],
        out_specs=(vmem, vmem),
        scratch_shapes=[pltpu.VMEM((CACHE, n * HD), jnp.bfloat16) for n in CHUNKS]
        + [pltpu.VMEM((N_GRP, TILE, n * HD), jnp.bfloat16) for n in CHUNKS] * 2
        + [
            pltpu.VMEM((CACHE, GW), jnp.bfloat16),
            pltpu.VMEM((STEPS, GW), jnp.bfloat16),
            pltpu.VMEM((N_W, FEAT, WCHUNK), jnp.bfloat16),
            pltpu.SMEM((N_GRP,), jnp.int32),
            pltpu.VMEM((1, HD), jnp.int32),
            pltpu.SMEM((1, HD), jnp.int32),
            pltpu.VMEM((PAD, GW), jnp.float32),
            pltpu.VMEM((PAD, FEAT), jnp.bfloat16),
            pltpu.VMEM((PAD, D), jnp.float32),
            pltpu.VMEM((N_ULYS, PAD, FEAT), jnp.float32),
            pltpu.SemaphoreType.DMA((N_B,)),
            pltpu.SemaphoreType.DMA((N_W,)),
            pltpu.SemaphoreType.DMA((2,)),
        ]
        + [pltpu.SemaphoreType.DMA((N_C,))] * 4
        + [pltpu.SemaphoreType.DMA] * 2,
        compiler_params=pltpu.CompilerParams(
            vmem_limit_bytes=VLIM * MIB, collective_id=0, has_side_effects=True
        ),
        name="step",
    )(
        pinned(layer_states), pinned(new_states.reshape(STEPS, GW)), pinned(out_proj),
        lengths, finished, pinned(assignment),
    )
    decoded, scored = pl.pallas_call(
        norm_kernel,
        out_shape=(
            jax.ShapeDtypeStruct((STEPS, FEAT), jnp.bfloat16),
            jax.ShapeDtypeStruct((PBLK, D), jnp.bfloat16),
        ),
        in_specs=[vmem] * 3,
        out_specs=(hbm, hbm),
        scratch_shapes=[pltpu.VMEM((PBLK, D), jnp.bfloat16), pltpu.SemaphoreType.DMA((N_Y + 1,))],
        compiler_params=pltpu.CompilerParams(vmem_limit_bytes=8 * MIB),
        name="norm",
    )(raw, dec, gain.reshape(D // HD, HD))
    return (decoded.reshape(STEPS, 1, FEAT), scored.reshape(1, PBLK, D))


def solution(mesh):
    placed = (
        P("grp", None, "ulys"),
        P(None, "grp", "ulys"),
        P("ulys", None),
        P(),
        P("grp"),
        P("grp"),
        P(),
    )
    return jax.shard_map(
        body,
        mesh=mesh,
        in_specs=placed,
        out_specs=(P(None, "grp", "ulys"), P("grp", "ulys", None)),
        check_vma=False,
    )
```

```python
import math

import jax
import jax.numpy as jnp
from jax import lax
from jax.experimental import pallas as pl
from jax.experimental.pallas import tpu as pltpu
from jax.sharding import PartitionSpec as P

HD = 128
QPK = 5
GW = 896
FEAT = QPK * HD
CACHE = 512
D = 5120
STEPS = 3
N_GRP = 32
N_ULYS = 8
N_Z = 8
N_Y = 4
PBLK = CACHE // N_ULYS
TILE = PBLK // N_Y
QBLK = 128
N_B = CACHE // QBLK
B_TILES = QBLK // TILE
PAD = 8
WCHUNK = 1280
N_W = D // WCHUNK
EXP2_SCALE = HD ** (-0.5) * math.log2(math.e)
NEG = -1e30
MIB = 1024 * 1024
MESH = pl.DeviceIdType.MESH
CHUNKS = (2, 3)


FIRST = tuple(sum(CHUNKS[:c]) for c in range(len(CHUNKS)))
N_C = len(CHUNKS)


def div(a, n):
    return lax.div(a, jnp.int32(n))


def rem(a, n):
    return lax.rem(a, jnp.int32(n))


def relay_of(head, b, i):
    p = 2 * b + div(i, N_Y)
    return rem(head + p, N_Z) * N_Y + rem(b + i, N_Y), p


def tile_of(z, y, u):
    b = u // 2
    r = (y - b + N_Y) % N_Y
    return (z - u + N_Z) % N_Z, b, (u % 2) * N_Y + r


def attend_block(x, out, b, first, count, limit):
    rows = lax.broadcasted_iota(jnp.int32, (QBLK, 1), 0)
    cols = lax.broadcasted_iota(jnp.int32, (1, QBLK), 1)
    top = b * QBLK
    span = top + QBLK
    keys = x[0:span, FEAT:FEAT + HD]
    values = x[0:span, FEAT + HD:FEAT + 2 * HD]
    live = rows + top < limit
    for j in range(count):
        q = first + j
        query = x[top:span, q * HD:(q + 1) * HD]
        s = lax.dot_general(query, keys, (((1,), (1,)), ((), ())), preferred_element_type=jnp.float32)
        diag = jnp.where(cols <= rows, s[:, top:span], NEG)
        s = diag if b == 0 else jnp.concatenate([s[:, :top], diag], axis=1)
        m = jnp.max(s, axis=1, keepdims=True)
        p = jnp.exp2((s - m) * EXP2_SCALE)
        total = jnp.sum(p, axis=1, keepdims=True)
        o = jnp.dot(p.astype(jnp.bfloat16), values, preferred_element_type=jnp.float32)
        o = jnp.where(live, o * (1.0 / total), 0.0)
        out[top:span, j * HD:(j + 1) * HD] = o.astype(jnp.bfloat16)


def decode_heads(x, fresh, dhead, length):
    keys = x[:, FEAT:FEAT + HD]
    values = x[:, FEAT + HD:FEAT + 2 * HD]
    new_keys = fresh[:, FEAT:FEAT + HD].astype(jnp.bfloat16)
    new_values = fresh[:, FEAT + HD:FEAT + 2 * HD].astype(jnp.bfloat16)
    old_mask = lax.broadcasted_iota(jnp.int32, (1, CACHE), 1) < length
    step = lax.broadcasted_iota(jnp.int32, (PAD, PAD), 0)
    new_mask = lax.broadcasted_iota(jnp.int32, (PAD, PAD), 1) <= step
    dims = (((1,), (1,)), ((), ()))
    for q in range(QPK):
        query = fresh[:, q * HD:(q + 1) * HD].astype(jnp.bfloat16)
        old = lax.dot_general(query, keys, dims, preferred_element_type=jnp.float32)
        new = lax.dot_general(query, new_keys, dims, preferred_element_type=jnp.float32)
        old = jnp.where(old_mask, old, NEG)
        new = jnp.where(new_mask, new, NEG)
        m = jnp.maximum(jnp.max(old, axis=1, keepdims=True), jnp.max(new, axis=1, keepdims=True))
        p_old = jnp.exp2((old - m) * EXP2_SCALE)
        p_new = jnp.exp2((new - m) * EXP2_SCALE)
        total = jnp.sum(p_old, axis=1, keepdims=True) + jnp.sum(p_new, axis=1, keepdims=True)
        o = jnp.dot(p_old.astype(jnp.bfloat16), values, preferred_element_type=jnp.float32)
        o = o + jnp.dot(p_new.astype(jnp.bfloat16), new_values, preferred_element_type=jnp.float32)
        dhead[:, q * HD:(q + 1) * HD] = (o * (1.0 / total)).astype(jnp.bfloat16)


def step_kernel(x_hbm, new_hbm, w_hbm, length_s, done_s, assign_hbm, dec, raw, *scratch):
    heads, recv, stage = scratch[:N_C], scratch[N_C:2 * N_C], scratch[2 * N_C:3 * N_C]
    (x, new, w, assign, found, source, fresh, dhead, part, dec_in,
     x_sem, w_sem, small_sem, send1, recv1, send2, recv2, send3, recv3) = scratch[3 * N_C:]
    me = lax.axis_index("grp")
    u = lax.axis_index("ulys")
    z = me // N_Y
    y = me % N_Y
    g_in, _, i_in = tile_of(z, y, u)
    r_out = i_in % N_Y
    hit1 = jnp.where(g_in == u, 1, 0)

    small = [
        pltpu.make_async_copy(src, dst, small_sem.at[k])
        for k, (src, dst) in enumerate(
            ((assign_hbm, assign), (new_hbm, new)))
    ]
    x_copies = [
        pltpu.make_async_copy(x_hbm.at[0, pl.ds(b * QBLK, QBLK)], x.at[pl.ds(b * QBLK, QBLK)], x_sem.at[b])
        for b in range(N_B)
    ]
    w_copies = [
        pltpu.make_async_copy(w_hbm.at[:, pl.ds(c * WCHUNK, WCHUNK)], w.at[c], w_sem.at[c]) for c in range(N_W)
    ]
    for copy in x_copies:
        copy.start()

    barrier = pltpu.get_barrier_semaphore()

    def greet(grp, ulys):
        pl.semaphore_signal(barrier, inc=1, device_id=(grp, ulys), device_id_type=MESH)

    @pl.loop(1, N_GRP, unroll=True)
    def _(k):
        greet(rem(me + k, N_GRP), g_in)

    @pl.loop(1, N_ULYS, unroll=True)
    def _(k):
        greet(me, rem(u + k, N_ULYS))

    @pl.when(g_in != u)
    def _():
        greet(me, g_in)

    for copy in small + w_copies:
        copy.start()

    length = length_s[0]
    done = done_s[0]
    limit = length * done

    for c in range(N_C):
        for b in range(N_B):
            if c == 0:
                x_copies[b].wait()
            attend_block(x, heads[c], b, FIRST[c], CHUNKS[c], limit)
        if c == 0:
            pl.semaphore_wait(barrier, N_GRP - hit1 + N_ULYS - 1)

        @pl.loop(0, N_GRP)
        def _(k, c=c):
            b = rem(div(k, B_TILES) + z + y, N_B)
            i = rem(k + y + z, B_TILES)
            grp, ulys = relay_of(u, b, i)
            src = heads[c].at[pl.ds(pl.multiple_of(b * QBLK + i * TILE, TILE), TILE)]
            own = (grp == me) & (ulys == u)

            @pl.when(own)
            def _():
                pltpu.make_async_copy(src, recv[c].at[me], recv1.at[c]).start()

            @pl.when(jnp.logical_not(own))
            def _():
                pltpu.make_async_remote_copy(
                    src, recv[c].at[me], send1.at[c], recv1.at[c], device_id=(grp, ulys), device_id_type=MESH
                ).start()

    small[0].wait()
    place = lax.broadcasted_iota(jnp.int32, (N_GRP, HD), 0)
    group = jnp.zeros((N_GRP, HD), jnp.int32)
    for n in range(N_GRP):
        group = jnp.where(place == n, assign[n], group)
    lanes = lax.broadcasted_iota(jnp.int32, (N_GRP, HD), 1)
    found[...] = jnp.max(jnp.where(group == lanes, place, 0), axis=0, keepdims=True)
    to_scalars = pltpu.make_async_copy(found, source, small_sem.at[0])
    to_scalars.start()
    to_scalars.wait()

    rows = pl.ds(pl.multiple_of(r_out * TILE, TILE), TILE)
    for c in range(N_C):
        width = CHUNKS[c] * HD
        cols = pl.ds(pl.multiple_of(g_in * FEAT + FIRST[c] * HD, HD), width)
        pltpu.make_async_copy(recv[c], recv[c], recv1.at[c]).wait()

        @pl.loop(0, N_GRP - 1)
        def _(k, c=c, cols=cols):
            t = rem(k, N_Z) * N_Y + div(k, N_Z) if c + 1 < N_C else k
            t = jnp.where(t == me, N_GRP - 1, t)
            stage[c][t] = recv[c][source[0, t]]
            pltpu.make_async_remote_copy(
                stage[c].at[t], raw.at[rows, cols], send2.at[c], recv2.at[c], device_id=(t, u), device_id_type=MESH
            ).start()

        stage[c][me] = recv[c][source[0, me]]
        pltpu.make_async_copy(stage[c].at[me], raw.at[rows, cols], recv2.at[c]).start()

        if c > 0:
            continue
        small[1].wait()
        fresh[...] = jnp.zeros_like(fresh)
        fresh[0:STEPS, :] = new[...].astype(jnp.float32)
        decode_heads(x, fresh, dhead, length)
        lhs = dhead[...]
        for k in range(N_W):
            w_copies[k].wait()
            part[:, k * WCHUNK:(k + 1) * WCHUNK] = jnp.dot(lhs, w[k], preferred_element_type=jnp.float32)

        @pl.loop(1, N_ULYS)
        def _(k):
            p = rem(u + k, N_ULYS)
            pltpu.make_async_remote_copy(
                part.at[:, pl.ds(pl.multiple_of(p * FEAT, HD), FEAT)],
                dec_in.at[u], send3, recv3, device_id=(me, p), device_id_type=MESH
            ).start()

        pltpu.make_async_copy(part.at[:, pl.ds(pl.multiple_of(u * FEAT, HD), FEAT)], dec_in.at[u], recv3).start()

    pltpu.make_async_copy(dec_in, dec_in, recv3).wait()
    total = dec_in[0]
    for g in range(1, N_ULYS):
        total = total + dec_in[g]
    dec[...] = (total * (1 - done).astype(jnp.float32))[0:STEPS].astype(jnp.bfloat16)

    for c in range(N_C):
        pltpu.make_async_copy(recv[c], recv[c], recv2.at[c]).wait()
    for c in range(N_C):
        sent = stage[c].at[pl.ds(0, N_GRP - 1)]
        pltpu.make_async_copy(sent, sent, send2.at[c]).wait()

        @pl.when(hit1 > 0)
        def _(c=c, sent=sent):
            pltpu.make_async_copy(sent, sent, send1.at[c]).wait()

        @pl.when(hit1 <= 0)
        def _(c=c):
            pltpu.make_async_copy(stage[c], stage[c], send1.at[c]).wait()

    sent = dec_in.at[pl.ds(0, N_ULYS - 1)]
    pltpu.make_async_copy(sent, sent, send3).wait()


def norm_kernel(raw, dec, gain, decoded, scored, out, sem):
    copies = [pltpu.make_async_copy(dec, decoded, sem.at[N_Y])]
    copies[0].start()
    gains = gain[...].astype(jnp.float32)
    for r in range(N_Y):
        rows = slice(r * TILE, (r + 1) * TILE)
        square = jnp.zeros((TILE, HD), jnp.float32)
        for k in range(D // HD):
            lifted = raw[rows, k * HD:(k + 1) * HD].astype(jnp.float32)
            square = square + lifted * lifted
        power = jnp.sum(square, axis=1, keepdims=True) * (1.0 / D)
        factor = lax.rsqrt(power + 1e-06)
        for k in range(D // HD):
            lifted = raw[rows, k * HD:(k + 1) * HD].astype(jnp.float32)
            out[rows, k * HD:(k + 1) * HD] = (lifted * factor * gains[k:k + 1]).astype(jnp.bfloat16)
        at = pl.ds(r * TILE, TILE)
        copies.append(pltpu.make_async_copy(out.at[at], scored.at[at], sem.at[r]))
        copies[-1].start()
    for copy in copies:
        copy.wait()


def body(layer_states, new_states, out_proj, gain, lengths, finished, assignment):
    hbm = pl.BlockSpec(memory_space=pl.ANY)
    vmem = pl.BlockSpec(memory_space=pltpu.VMEM)
    smem = pl.BlockSpec(memory_space=pltpu.SMEM)

    def pinned(a):
        return pltpu.with_memory_space_constraint(a, pltpu.HBM)

    dec, raw = pl.pallas_call(
        step_kernel,
        out_shape=(
            pltpu.VMEM((STEPS, FEAT), jnp.bfloat16),
            pltpu.VMEM((PBLK, D), jnp.bfloat16),
        ),
        in_specs=[hbm] * 3 + [smem] * 2 + [hbm],
        out_specs=(vmem, vmem),
        scratch_shapes=[pltpu.VMEM((CACHE, n * HD), jnp.bfloat16) for n in CHUNKS]
        + [pltpu.VMEM((N_GRP, TILE, n * HD), jnp.bfloat16) for n in CHUNKS] * 2
        + [
            pltpu.VMEM((CACHE, GW), jnp.bfloat16),
            pltpu.VMEM((STEPS, GW), jnp.bfloat16),
            pltpu.VMEM((N_W, FEAT, WCHUNK), jnp.bfloat16),
            pltpu.SMEM((N_GRP,), jnp.int32),
            pltpu.VMEM((1, HD), jnp.int32),
            pltpu.SMEM((1, HD), jnp.int32),
            pltpu.VMEM((PAD, GW), jnp.float32),
            pltpu.VMEM((PAD, FEAT), jnp.bfloat16),
            pltpu.VMEM((PAD, D), jnp.float32),
            pltpu.VMEM((N_ULYS, PAD, FEAT), jnp.float32),
            pltpu.SemaphoreType.DMA((N_B,)),
            pltpu.SemaphoreType.DMA((N_W,)),
            pltpu.SemaphoreType.DMA((2,)),
        ]
        + [pltpu.SemaphoreType.DMA((N_C,))] * 4
        + [pltpu.SemaphoreType.DMA] * 2,
        compiler_params=pltpu.CompilerParams(
            vmem_limit_bytes=32 * MIB, collective_id=0, has_side_effects=True
        ),
        name="step",
    )(
        pinned(layer_states), pinned(new_states.reshape(STEPS, GW)), pinned(out_proj),
        lengths, finished, pinned(assignment),
    )
    decoded, scored = pl.pallas_call(
        norm_kernel,
        out_shape=(
            jax.ShapeDtypeStruct((STEPS, FEAT), jnp.bfloat16),
            jax.ShapeDtypeStruct((PBLK, D), jnp.bfloat16),
        ),
        in_specs=[vmem] * 3,
        out_specs=(hbm, hbm),
        scratch_shapes=[pltpu.VMEM((PBLK, D), jnp.bfloat16), pltpu.SemaphoreType.DMA((N_Y + 1,))],
        compiler_params=pltpu.CompilerParams(vmem_limit_bytes=8 * MIB),
        name="norm",
    )(raw, dec, gain.reshape(D // HD, HD))
    return (decoded.reshape(STEPS, 1, FEAT), scored.reshape(1, PBLK, D))


def solution(mesh):
    placed = (
        P("grp", None, "ulys"),
        P(None, "grp", "ulys"),
        P("ulys", None),
        P(),
        P("grp"),
        P("grp"),
        P(),
    )
    return jax.shard_map(
        body,
        mesh=mesh,
        in_specs=placed,
        out_specs=(P(None, "grp", "ulys"), P("grp", "ulys", None)),
        check_vma=False,
    )
```

```python
import math

import jax
import jax.numpy as jnp
from jax import lax
from jax.experimental import pallas as pl
from jax.experimental.pallas import tpu as pltpu
from jax.sharding import PartitionSpec as P

HD = 128
QPK = 5
GW = 896
FEAT = QPK * HD
CACHE = 512
D = 5120
STEPS = 3
N_GRP = 32
N_ULYS = 8
N_Z = 8
N_Y = 4
PBLK = CACHE // N_ULYS
TILE = PBLK // N_Y
QBLK = 128
N_B = CACHE // QBLK
B_TILES = QBLK // TILE
PAD = 8
WCHUNK = 1280
N_W = D // WCHUNK
EXP2_SCALE = HD ** (-0.5) * math.log2(math.e)
NEG = -1e30
MIB = 1024 * 1024
MESH = pl.DeviceIdType.MESH
CHUNKS = (2, 3)


FIRST = tuple(sum(CHUNKS[:c]) for c in range(len(CHUNKS)))
N_C = len(CHUNKS)
ORDER = (0, 1, 4, 2, 5, 8, 3, 6, 9, 7, 10, 11, 12, 13, 14, 15, 28, 29, 30, 31, 24, 25, 26, 27, 16, 17, 18, 19, 20, 21, 22)
ORDER_LAST = 23


def div(a, n):
    return lax.div(a, jnp.int32(n))


def rem(a, n):
    return lax.rem(a, jnp.int32(n))


def relay_of(head, b, i):
    p = 2 * b + div(i, N_Y)
    return rem(head + p, N_Z) * N_Y + rem(b + i, N_Y), p


def tile_of(z, y, u):
    b = u // 2
    r = (y - b + N_Y) % N_Y
    return (z - u + N_Z) % N_Z, b, (u % 2) * N_Y + r


def attend_block(x, out, b, first, count, limit):
    rows = lax.broadcasted_iota(jnp.int32, (QBLK, 1), 0)
    cols = lax.broadcasted_iota(jnp.int32, (1, QBLK), 1)
    top = b * QBLK
    span = top + QBLK
    keys = x[0:span, FEAT:FEAT + HD]
    values = x[0:span, FEAT + HD:FEAT + 2 * HD]
    live = rows + top < limit
    for j in range(count):
        q = first + j
        query = x[top:span, q * HD:(q + 1) * HD]
        s = lax.dot_general(query, keys, (((1,), (1,)), ((), ())), preferred_element_type=jnp.float32)
        diag = jnp.where(cols <= rows, s[:, top:span], NEG)
        s = diag if b == 0 else jnp.concatenate([s[:, :top], diag], axis=1)
        m = jnp.max(s, axis=1, keepdims=True)
        p = jnp.exp2((s - m) * EXP2_SCALE)
        total = jnp.sum(p, axis=1, keepdims=True)
        o = jnp.dot(p.astype(jnp.bfloat16), values, preferred_element_type=jnp.float32)
        o = jnp.where(live, o * (1.0 / total), 0.0)
        out[top:span, j * HD:(j + 1) * HD] = o.astype(jnp.bfloat16)


def decode_heads(x, fresh, dhead, length):
    keys = x[:, FEAT:FEAT + HD]
    values = x[:, FEAT + HD:FEAT + 2 * HD]
    new_keys = fresh[:, FEAT:FEAT + HD].astype(jnp.bfloat16)
    new_values = fresh[:, FEAT + HD:FEAT + 2 * HD].astype(jnp.bfloat16)
    old_mask = lax.broadcasted_iota(jnp.int32, (1, CACHE), 1) < length
    step = lax.broadcasted_iota(jnp.int32, (PAD, PAD), 0)
    new_mask = lax.broadcasted_iota(jnp.int32, (PAD, PAD), 1) <= step
    dims = (((1,), (1,)), ((), ()))
    for q in range(QPK):
        query = fresh[:, q * HD:(q + 1) * HD].astype(jnp.bfloat16)
        old = lax.dot_general(query, keys, dims, preferred_element_type=jnp.float32)
        new = lax.dot_general(query, new_keys, dims, preferred_element_type=jnp.float32)
        old = jnp.where(old_mask, old, NEG)
        new = jnp.where(new_mask, new, NEG)
        m = jnp.maximum(jnp.max(old, axis=1, keepdims=True), jnp.max(new, axis=1, keepdims=True))
        p_old = jnp.exp2((old - m) * EXP2_SCALE)
        p_new = jnp.exp2((new - m) * EXP2_SCALE)
        total = jnp.sum(p_old, axis=1, keepdims=True) + jnp.sum(p_new, axis=1, keepdims=True)
        o = jnp.dot(p_old.astype(jnp.bfloat16), values, preferred_element_type=jnp.float32)
        o = o + jnp.dot(p_new.astype(jnp.bfloat16), new_values, preferred_element_type=jnp.float32)
        dhead[:, q * HD:(q + 1) * HD] = (o * (1.0 / total)).astype(jnp.bfloat16)


def step_kernel(x_hbm, new_hbm, w_hbm, length_s, done_s, assign_hbm, dec, *buffers):
    raw, scratch = buffers[:N_C], buffers[N_C:]
    heads, recv, stage = scratch[:N_C], scratch[N_C:2 * N_C], scratch[2 * N_C:3 * N_C]
    (x, new, w, assign, found, source, fresh, dhead, part, dec_in,
     x_sem, w_sem, small_sem, send1, recv1, send2, recv2, send3, recv3) = scratch[3 * N_C:]
    me = lax.axis_index("grp")
    u = lax.axis_index("ulys")
    z = me // N_Y
    y = me % N_Y
    g_in, _, i_in = tile_of(z, y, u)
    r_out = i_in % N_Y
    hit1 = jnp.where(g_in == u, 1, 0)

    small = [
        pltpu.make_async_copy(src, dst, small_sem.at[k])
        for k, (src, dst) in enumerate(
            ((assign_hbm, assign), (new_hbm, new)))
    ]
    x_copies = [
        pltpu.make_async_copy(x_hbm.at[0, pl.ds(b * QBLK, QBLK)], x.at[pl.ds(b * QBLK, QBLK)], x_sem.at[b])
        for b in range(N_B)
    ]
    w_copies = [
        pltpu.make_async_copy(w_hbm.at[:, pl.ds(c * WCHUNK, WCHUNK)], w.at[c], w_sem.at[c]) for c in range(N_W)
    ]
    for copy in x_copies:
        copy.start()

    barrier = pltpu.get_barrier_semaphore()

    def greet(grp, ulys):
        pl.semaphore_signal(barrier, inc=1, device_id=(grp, ulys), device_id_type=MESH)

    @pl.loop(1, N_GRP, unroll=True)
    def _(k):
        greet(rem(me + k, N_GRP), g_in)

    @pl.loop(1, N_ULYS, unroll=True)
    def _(k):
        greet(me, rem(u + k, N_ULYS))

    @pl.when(g_in != u)
    def _():
        greet(me, g_in)

    for copy in small + w_copies:
        copy.start()

    length = length_s[0]
    done = done_s[0]
    limit = length * done

    for c in range(N_C):
        for b in range(N_B):
            if c == 0:
                x_copies[b].wait()
            attend_block(x, heads[c], b, FIRST[c], CHUNKS[c], limit)
        if c == 0:
            pl.semaphore_wait(barrier, N_GRP - hit1 + N_ULYS - 1)

        @pl.loop(0, N_GRP)
        def _(k, c=c):
            b = rem(div(k, B_TILES) + z + y, N_B)
            i = rem(k + y + z, B_TILES)
            grp, ulys = relay_of(u, b, i)
            src = heads[c].at[pl.ds(pl.multiple_of(b * QBLK + i * TILE, TILE), TILE)]
            own = (grp == me) & (ulys == u)

            @pl.when(own)
            def _():
                pltpu.make_async_copy(src, recv[c].at[me], recv1.at[c]).start()

            @pl.when(jnp.logical_not(own))
            def _():
                pltpu.make_async_remote_copy(
                    src, recv[c].at[me], send1.at[c], recv1.at[c], device_id=(grp, ulys), device_id_type=MESH
                ).start()

    small[0].wait()
    place = lax.broadcasted_iota(jnp.int32, (N_GRP, HD), 0)
    group = jnp.zeros((N_GRP, HD), jnp.int32)
    for n in range(N_GRP):
        group = jnp.where(place == n, assign[n], group)
    lanes = lax.broadcasted_iota(jnp.int32, (N_GRP, HD), 1)
    found[...] = jnp.max(jnp.where(group == lanes, place, 0), axis=0, keepdims=True)
    to_scalars = pltpu.make_async_copy(found, source, small_sem.at[0])
    to_scalars.start()
    to_scalars.wait()

    slot = g_in * N_Y + r_out
    for c in range(N_C):
        pltpu.make_async_copy(recv[c], recv[c], recv1.at[c]).wait()

        def forward(t, c=c):
            stage[c][t] = recv[c][source[0, t]]
            pltpu.make_async_remote_copy(
                stage[c].at[t], raw[c].at[slot], send2.at[c], recv2.at[c], device_id=(t, u), device_id_type=MESH
            ).start()

        if c + 1 < N_C:
            @pl.loop(0, N_GRP - 1)
            def _(k):
                t = rem(k, N_Z) * N_Y + div(k, N_Z)
                forward(jnp.where(t == me, N_GRP - 1, t))
        else:
            for t in ORDER:
                forward(jnp.where(me == t, ORDER_LAST, t))

        stage[c][me] = recv[c][source[0, me]]
        pltpu.make_async_copy(stage[c].at[me], raw[c].at[slot], recv2.at[c]).start()

        if c > 0:
            continue
        small[1].wait()
        fresh[...] = jnp.zeros_like(fresh)
        fresh[0:STEPS, :] = new[...].astype(jnp.float32)
        decode_heads(x, fresh, dhead, length)
        lhs = dhead[...]
        for k in range(N_W):
            w_copies[k].wait()
            part[:, k * WCHUNK:(k + 1) * WCHUNK] = jnp.dot(lhs, w[k], preferred_element_type=jnp.float32)

        @pl.loop(1, N_ULYS)
        def _(k):
            p = rem(u + k, N_ULYS)
            pltpu.make_async_remote_copy(
                part.at[:, pl.ds(pl.multiple_of(p * FEAT, HD), FEAT)],
                dec_in.at[u], send3, recv3, device_id=(me, p), device_id_type=MESH
            ).start()

        pltpu.make_async_copy(part.at[:, pl.ds(pl.multiple_of(u * FEAT, HD), FEAT)], dec_in.at[u], recv3).start()

    pltpu.make_async_copy(dec_in, dec_in, recv3).wait()
    total = dec_in[0]
    for g in range(1, N_ULYS):
        total = total + dec_in[g]
    dec[...] = (total * (1 - done).astype(jnp.float32))[0:STEPS].astype(jnp.bfloat16)

    for c in range(N_C):
        pltpu.make_async_copy(recv[c], recv[c], recv2.at[c]).wait()
    for c in range(N_C):
        sent = stage[c].at[pl.ds(0, N_GRP - 1)]
        pltpu.make_async_copy(sent, sent, send2.at[c]).wait()

        @pl.when(hit1 > 0)
        def _(c=c, sent=sent):
            pltpu.make_async_copy(sent, sent, send1.at[c]).wait()

        @pl.when(hit1 <= 0)
        def _(c=c):
            pltpu.make_async_copy(stage[c], stage[c], send1.at[c]).wait()

    sent = dec_in.at[pl.ds(0, N_ULYS - 1)]
    pltpu.make_async_copy(sent, sent, send3).wait()


def norm_kernel(*refs):
    raw = refs[:N_C]
    dec, gain, decoded, scored, out, sem = refs[N_C:]
    copies = [pltpu.make_async_copy(dec, decoded, sem.at[N_Y])]
    copies[0].start()
    gains = gain[...].astype(jnp.float32)
    places = [(g, c, j) for g in range(N_ULYS) for c in range(N_C) for j in range(CHUNKS[c])]
    for r in range(N_Y):
        rows = slice(r * TILE, (r + 1) * TILE)
        square = jnp.zeros((TILE, HD), jnp.float32)
        for g, c, j in places:
            lifted = raw[c][g * N_Y + r, :, j * HD:(j + 1) * HD].astype(jnp.float32)
            square = square + lifted * lifted
        power = jnp.sum(square, axis=1, keepdims=True) * (1.0 / D)
        factor = lax.rsqrt(power + 1e-06)
        for k, (g, c, j) in enumerate(places):
            lifted = raw[c][g * N_Y + r, :, j * HD:(j + 1) * HD].astype(jnp.float32)
            out[rows, k * HD:(k + 1) * HD] = (lifted * factor * gains[k:k + 1]).astype(jnp.bfloat16)
        at = pl.ds(r * TILE, TILE)
        copies.append(pltpu.make_async_copy(out.at[at], scored.at[at], sem.at[r]))
        copies[-1].start()
    for copy in copies:
        copy.wait()


def body(layer_states, new_states, out_proj, gain, lengths, finished, assignment):
    hbm = pl.BlockSpec(memory_space=pl.ANY)
    vmem = pl.BlockSpec(memory_space=pltpu.VMEM)
    smem = pl.BlockSpec(memory_space=pltpu.SMEM)

    def pinned(a):
        return pltpu.with_memory_space_constraint(a, pltpu.HBM)

    dec, *raw = pl.pallas_call(
        step_kernel,
        out_shape=(
            pltpu.VMEM((STEPS, FEAT), jnp.bfloat16),
        ) + tuple(pltpu.VMEM((N_GRP, TILE, n * HD), jnp.bfloat16) for n in CHUNKS),
        in_specs=[hbm] * 3 + [smem] * 2 + [hbm],
        out_specs=(vmem,) * (1 + N_C),
        scratch_shapes=[pltpu.VMEM((CACHE, n * HD), jnp.bfloat16) for n in CHUNKS]
        + [pltpu.VMEM((N_GRP, TILE, n * HD), jnp.bfloat16) for n in CHUNKS] * 2
        + [
            pltpu.VMEM((CACHE, GW), jnp.bfloat16),
            pltpu.VMEM((STEPS, GW), jnp.bfloat16),
            pltpu.VMEM((N_W, FEAT, WCHUNK), jnp.bfloat16),
            pltpu.SMEM((N_GRP,), jnp.int32),
            pltpu.VMEM((1, HD), jnp.int32),
            pltpu.SMEM((1, HD), jnp.int32),
            pltpu.VMEM((PAD, GW), jnp.float32),
            pltpu.VMEM((PAD, FEAT), jnp.bfloat16),
            pltpu.VMEM((PAD, D), jnp.float32),
            pltpu.VMEM((N_ULYS, PAD, FEAT), jnp.float32),
            pltpu.SemaphoreType.DMA((N_B,)),
            pltpu.SemaphoreType.DMA((N_W,)),
            pltpu.SemaphoreType.DMA((2,)),
        ]
        + [pltpu.SemaphoreType.DMA((N_C,))] * 4
        + [pltpu.SemaphoreType.DMA] * 2,
        compiler_params=pltpu.CompilerParams(
            vmem_limit_bytes=32 * MIB, collective_id=0, has_side_effects=True
        ),
        name="step",
    )(
        pinned(layer_states), pinned(new_states.reshape(STEPS, GW)), pinned(out_proj),
        lengths, finished, pinned(assignment),
    )
    decoded, scored = pl.pallas_call(
        norm_kernel,
        out_shape=(
            jax.ShapeDtypeStruct((STEPS, FEAT), jnp.bfloat16),
            jax.ShapeDtypeStruct((PBLK, D), jnp.bfloat16),
        ),
        in_specs=[vmem] * (2 + N_C),
        out_specs=(hbm, hbm),
        scratch_shapes=[pltpu.VMEM((PBLK, D), jnp.bfloat16), pltpu.SemaphoreType.DMA((N_Y + 1,))],
        compiler_params=pltpu.CompilerParams(vmem_limit_bytes=8 * MIB),
        name="norm",
    )(*raw, dec, gain.reshape(D // HD, HD))
    return (decoded.reshape(STEPS, 1, FEAT), scored.reshape(1, PBLK, D))


def solution(mesh):
    placed = (
        P("grp", None, "ulys"),
        P(None, "grp", "ulys"),
        P("ulys", None),
        P(),
        P("grp"),
        P("grp"),
        P(),
    )
    return jax.shard_map(
        body,
        mesh=mesh,
        in_specs=placed,
        out_specs=(P(None, "grp", "ulys"), P("grp", "ulys", None)),
        check_vma=False,
    )
```

```python
import math

import jax
import jax.numpy as jnp
from jax import lax
from jax.experimental import pallas as pl
from jax.experimental.pallas import tpu as pltpu
from jax.sharding import PartitionSpec as P

HD = 128
QPK = 5
GW = 896
FEAT = QPK * HD
CACHE = 512
D = 5120
STEPS = 3
N_GRP = 32
N_ULYS = 8
N_Z = 8
N_Y = 4
PBLK = CACHE // N_ULYS
TILE = PBLK // N_Y
QBLK = 128
N_B = CACHE // QBLK
B_TILES = QBLK // TILE
PAD = 8
WCHUNK = 1280
N_W = D // WCHUNK
EXP2_SCALE = HD ** (-0.5) * math.log2(math.e)
NEG = -1e30
MIB = 1024 * 1024
MESH = pl.DeviceIdType.MESH
CHUNKS = (2, 3)


FIRST = tuple(sum(CHUNKS[:c]) for c in range(len(CHUNKS)))
N_C = len(CHUNKS)
ORDER = (0, 3, 4, 1, 7, 8, 2, 11, 5, 6, 9, 10, 12, 13, 14, 15, 28, 29, 30, 31, 24, 25, 26, 27, 16, 17, 18, 19, 20, 21, 22)
ORDER_LAST = 23


def div(a, n):
    return lax.div(a, jnp.int32(n))


def rem(a, n):
    return lax.rem(a, jnp.int32(n))


def relay_of(head, b, i):
    p = 2 * b + div(i, N_Y)
    return rem(head + p, N_Z) * N_Y + rem(b + i, N_Y), p


def tile_of(z, y, u):
    b = u // 2
    r = (y - b + N_Y) % N_Y
    return (z - u + N_Z) % N_Z, b, (u % 2) * N_Y + r


def attend_block(x, out, b, first, count, limit):
    rows = lax.broadcasted_iota(jnp.int32, (QBLK, 1), 0)
    cols = lax.broadcasted_iota(jnp.int32, (1, QBLK), 1)
    top = b * QBLK
    span = top + QBLK
    keys = x[0:span, FEAT:FEAT + HD]
    values = x[0:span, FEAT + HD:FEAT + 2 * HD]
    live = rows + top < limit
    for j in range(count):
        q = first + j
        query = x[top:span, q * HD:(q + 1) * HD]
        s = lax.dot_general(query, keys, (((1,), (1,)), ((), ())), preferred_element_type=jnp.float32)
        diag = jnp.where(cols <= rows, s[:, top:span], NEG)
        s = diag if b == 0 else jnp.concatenate([s[:, :top], diag], axis=1)
        m = jnp.max(s, axis=1, keepdims=True)
        p = jnp.exp2((s - m) * EXP2_SCALE)
        total = jnp.sum(p, axis=1, keepdims=True)
        o = jnp.dot(p.astype(jnp.bfloat16), values, preferred_element_type=jnp.float32)
        o = jnp.where(live, o * (1.0 / total), 0.0)
        out[top:span, j * HD:(j + 1) * HD] = o.astype(jnp.bfloat16)


def decode_heads(x, fresh, dhead, length):
    keys = x[:, FEAT:FEAT + HD]
    values = x[:, FEAT + HD:FEAT + 2 * HD]
    new_keys = fresh[:, FEAT:FEAT + HD].astype(jnp.bfloat16)
    new_values = fresh[:, FEAT + HD:FEAT + 2 * HD].astype(jnp.bfloat16)
    old_mask = lax.broadcasted_iota(jnp.int32, (1, CACHE), 1) < length
    step = lax.broadcasted_iota(jnp.int32, (PAD, PAD), 0)
    new_mask = lax.broadcasted_iota(jnp.int32, (PAD, PAD), 1) <= step
    dims = (((1,), (1,)), ((), ()))
    for q in range(QPK):
        query = fresh[:, q * HD:(q + 1) * HD].astype(jnp.bfloat16)
        old = lax.dot_general(query, keys, dims, preferred_element_type=jnp.float32)
        new = lax.dot_general(query, new_keys, dims, preferred_element_type=jnp.float32)
        old = jnp.where(old_mask, old, NEG)
        new = jnp.where(new_mask, new, NEG)
        m = jnp.maximum(jnp.max(old, axis=1, keepdims=True), jnp.max(new, axis=1, keepdims=True))
        p_old = jnp.exp2((old - m) * EXP2_SCALE)
        p_new = jnp.exp2((new - m) * EXP2_SCALE)
        total = jnp.sum(p_old, axis=1, keepdims=True) + jnp.sum(p_new, axis=1, keepdims=True)
        o = jnp.dot(p_old.astype(jnp.bfloat16), values, preferred_element_type=jnp.float32)
        o = o + jnp.dot(p_new.astype(jnp.bfloat16), new_values, preferred_element_type=jnp.float32)
        dhead[:, q * HD:(q + 1) * HD] = (o * (1.0 / total)).astype(jnp.bfloat16)


def step_kernel(x_hbm, new_hbm, w_hbm, length_s, done_s, assign_hbm, dec, squares, *buffers):
    raw, scratch = buffers[:N_C], buffers[N_C:]
    heads, recv, stage = scratch[:N_C], scratch[N_C:2 * N_C], scratch[2 * N_C:3 * N_C]
    (x, new, w, assign, found, source, fresh, dhead, part, dec_in,
     x_sem, w_sem, small_sem, send1, recv1, send2, recv2, send3, recv3) = scratch[3 * N_C:]
    me = lax.axis_index("grp")
    u = lax.axis_index("ulys")
    z = me // N_Y
    y = me % N_Y
    g_in, _, i_in = tile_of(z, y, u)
    r_out = i_in % N_Y
    hit1 = jnp.where(g_in == u, 1, 0)

    small = [
        pltpu.make_async_copy(src, dst, small_sem.at[k])
        for k, (src, dst) in enumerate(
            ((assign_hbm, assign), (new_hbm, new)))
    ]
    x_copies = [
        pltpu.make_async_copy(x_hbm.at[0, pl.ds(b * QBLK, QBLK)], x.at[pl.ds(b * QBLK, QBLK)], x_sem.at[b])
        for b in range(N_B)
    ]
    w_copies = [
        pltpu.make_async_copy(w_hbm.at[:, pl.ds(c * WCHUNK, WCHUNK)], w.at[c], w_sem.at[c]) for c in range(N_W)
    ]
    for copy in x_copies:
        copy.start()

    barrier = pltpu.get_barrier_semaphore()

    def greet(grp, ulys):
        pl.semaphore_signal(barrier, inc=1, device_id=(grp, ulys), device_id_type=MESH)

    @pl.loop(1, N_GRP, unroll=True)
    def _(k):
        greet(rem(me + k, N_GRP), g_in)

    @pl.loop(1, N_ULYS, unroll=True)
    def _(k):
        greet(me, rem(u + k, N_ULYS))

    @pl.when(g_in != u)
    def _():
        greet(me, g_in)

    for copy in small + w_copies:
        copy.start()

    length = length_s[0]
    done = done_s[0]
    limit = length * done

    for c in range(N_C):
        for b in range(N_B):
            if c == 0:
                x_copies[b].wait()
            attend_block(x, heads[c], b, FIRST[c], CHUNKS[c], limit)
        if c == 0:
            pl.semaphore_wait(barrier, N_GRP - hit1 + N_ULYS - 1)

        @pl.loop(0, N_GRP)
        def _(k, c=c):
            b = rem(div(k, B_TILES) + z + y, N_B)
            i = rem(k + y + z, B_TILES)
            grp, ulys = relay_of(u, b, i)
            src = heads[c].at[pl.ds(pl.multiple_of(b * QBLK + i * TILE, TILE), TILE)]
            own = (grp == me) & (ulys == u)

            @pl.when(own)
            def _():
                pltpu.make_async_copy(src, recv[c].at[me], recv1.at[c]).start()

            @pl.when(jnp.logical_not(own))
            def _():
                pltpu.make_async_remote_copy(
                    src, recv[c].at[me], send1.at[c], recv1.at[c], device_id=(grp, ulys), device_id_type=MESH
                ).start()

    small[0].wait()
    place = lax.broadcasted_iota(jnp.int32, (N_GRP, HD), 0)
    group = jnp.zeros((N_GRP, HD), jnp.int32)
    for n in range(N_GRP):
        group = jnp.where(place == n, assign[n], group)
    lanes = lax.broadcasted_iota(jnp.int32, (N_GRP, HD), 1)
    found[...] = jnp.max(jnp.where(group == lanes, place, 0), axis=0, keepdims=True)
    to_scalars = pltpu.make_async_copy(found, source, small_sem.at[0])
    to_scalars.start()
    to_scalars.wait()

    slot = g_in * N_Y + r_out
    for c in range(N_C):
        pltpu.make_async_copy(recv[c], recv[c], recv1.at[c]).wait()

        def forward(t, c=c):
            stage[c][t] = recv[c][source[0, t]]
            pltpu.make_async_remote_copy(
                stage[c].at[t], raw[c].at[slot], send2.at[c], recv2.at[c], device_id=(t, u), device_id_type=MESH
            ).start()

        if c + 1 < N_C:
            @pl.loop(0, N_GRP - 1)
            def _(k):
                t = rem(k, N_Z) * N_Y + div(k, N_Z)
                forward(jnp.where(t == me, N_GRP - 1, t))
        else:
            for t in ORDER:
                forward(jnp.where(me == t, ORDER_LAST, t))

        stage[c][me] = recv[c][source[0, me]]
        pltpu.make_async_copy(stage[c].at[me], raw[c].at[slot], recv2.at[c]).start()

        if c > 0:
            continue
        small[1].wait()
        fresh[...] = jnp.zeros_like(fresh)
        fresh[0:STEPS, :] = new[...].astype(jnp.float32)
        decode_heads(x, fresh, dhead, length)
        lhs = dhead[...]
        for k in range(N_W):
            w_copies[k].wait()
            part[:, k * WCHUNK:(k + 1) * WCHUNK] = jnp.dot(lhs, w[k], preferred_element_type=jnp.float32)

        @pl.loop(1, N_ULYS)
        def _(k):
            p = rem(u + k, N_ULYS)
            pltpu.make_async_remote_copy(
                part.at[:, pl.ds(pl.multiple_of(p * FEAT, HD), FEAT)],
                dec_in.at[u], send3, recv3, device_id=(me, p), device_id_type=MESH
            ).start()

        pltpu.make_async_copy(part.at[:, pl.ds(pl.multiple_of(u * FEAT, HD), FEAT)], dec_in.at[u], recv3).start()

    pltpu.make_async_copy(dec_in, dec_in, recv3).wait()
    total = dec_in[0]
    for g in range(1, N_ULYS):
        total = total + dec_in[g]
    dec[...] = (total * (1 - done).astype(jnp.float32))[0:STEPS].astype(jnp.bfloat16)

    for c in range(N_C):
        pltpu.make_async_copy(recv[c], recv[c], recv2.at[c]).wait()
        if c > 0:
            continue
        for r in range(N_Y):
            square = jnp.zeros((TILE, HD), jnp.float32)
            for g in range(N_ULYS):
                for j in range(CHUNKS[c]):
                    lifted = raw[c][g * N_Y + r, :, j * HD:(j + 1) * HD].astype(jnp.float32)
                    square = square + lifted * lifted
            squares[r * TILE:(r + 1) * TILE, :] = square
    for c in range(N_C):
        sent = stage[c].at[pl.ds(0, N_GRP - 1)]
        pltpu.make_async_copy(sent, sent, send2.at[c]).wait()

        @pl.when(hit1 > 0)
        def _(c=c, sent=sent):
            pltpu.make_async_copy(sent, sent, send1.at[c]).wait()

        @pl.when(hit1 <= 0)
        def _(c=c):
            pltpu.make_async_copy(stage[c], stage[c], send1.at[c]).wait()

    sent = dec_in.at[pl.ds(0, N_ULYS - 1)]
    pltpu.make_async_copy(sent, sent, send3).wait()


def norm_kernel(*refs):
    raw = refs[:N_C]
    dec, squares, gain, decoded, scored, out, sem = refs[N_C:]
    copies = [pltpu.make_async_copy(dec, decoded, sem.at[N_Y])]
    copies[0].start()
    gains = gain[...].astype(jnp.float32)
    places = [(g, c, j) for g in range(N_ULYS) for c in range(N_C) for j in range(CHUNKS[c])]
    for r in range(N_Y):
        rows = slice(r * TILE, (r + 1) * TILE)
        square = squares[rows, :]
        for g, c, j in places:
            if c == 0:
                continue
            lifted = raw[c][g * N_Y + r, :, j * HD:(j + 1) * HD].astype(jnp.float32)
            square = square + lifted * lifted
        power = jnp.sum(square, axis=1, keepdims=True) * (1.0 / D)
        factor = lax.rsqrt(power + 1e-06)
        for k, (g, c, j) in enumerate(places):
            lifted = raw[c][g * N_Y + r, :, j * HD:(j + 1) * HD].astype(jnp.float32)
            out[rows, k * HD:(k + 1) * HD] = (lifted * factor * gains[k:k + 1]).astype(jnp.bfloat16)
        at = pl.ds(r * TILE, TILE)
        copies.append(pltpu.make_async_copy(out.at[at], scored.at[at], sem.at[r]))
        copies[-1].start()
    for copy in copies:
        copy.wait()


def body(layer_states, new_states, out_proj, gain, lengths, finished, assignment):
    hbm = pl.BlockSpec(memory_space=pl.ANY)
    vmem = pl.BlockSpec(memory_space=pltpu.VMEM)
    smem = pl.BlockSpec(memory_space=pltpu.SMEM)

    def pinned(a):
        return pltpu.with_memory_space_constraint(a, pltpu.HBM)

    dec, squares, *raw = pl.pallas_call(
        step_kernel,
        out_shape=(
            pltpu.VMEM((STEPS, FEAT), jnp.bfloat16),
            pltpu.VMEM((PBLK, HD), jnp.float32),
        ) + tuple(pltpu.VMEM((N_GRP, TILE, n * HD), jnp.bfloat16) for n in CHUNKS),
        in_specs=[hbm] * 3 + [smem] * 2 + [hbm],
        out_specs=(vmem,) * (2 + N_C),
        scratch_shapes=[pltpu.VMEM((CACHE, n * HD), jnp.bfloat16) for n in CHUNKS]
        + [pltpu.VMEM((N_GRP, TILE, n * HD), jnp.bfloat16) for n in CHUNKS] * 2
        + [
            pltpu.VMEM((CACHE, GW), jnp.bfloat16),
            pltpu.VMEM((STEPS, GW), jnp.bfloat16),
            pltpu.VMEM((N_W, FEAT, WCHUNK), jnp.bfloat16),
            pltpu.SMEM((N_GRP,), jnp.int32),
            pltpu.VMEM((1, HD), jnp.int32),
            pltpu.SMEM((1, HD), jnp.int32),
            pltpu.VMEM((PAD, GW), jnp.float32),
            pltpu.VMEM((PAD, FEAT), jnp.bfloat16),
            pltpu.VMEM((PAD, D), jnp.float32),
            pltpu.VMEM((N_ULYS, PAD, FEAT), jnp.float32),
            pltpu.SemaphoreType.DMA((N_B,)),
            pltpu.SemaphoreType.DMA((N_W,)),
            pltpu.SemaphoreType.DMA((2,)),
        ]
        + [pltpu.SemaphoreType.DMA((N_C,))] * 4
        + [pltpu.SemaphoreType.DMA] * 2,
        compiler_params=pltpu.CompilerParams(
            vmem_limit_bytes=32 * MIB, collective_id=0, has_side_effects=True
        ),
        name="step",
    )(
        pinned(layer_states), pinned(new_states.reshape(STEPS, GW)), pinned(out_proj),
        lengths, finished, pinned(assignment),
    )
    decoded, scored = pl.pallas_call(
        norm_kernel,
        out_shape=(
            jax.ShapeDtypeStruct((STEPS, FEAT), jnp.bfloat16),
            jax.ShapeDtypeStruct((PBLK, D), jnp.bfloat16),
        ),
        in_specs=[vmem] * (3 + N_C),
        out_specs=(hbm, hbm),
        scratch_shapes=[pltpu.VMEM((PBLK, D), jnp.bfloat16), pltpu.SemaphoreType.DMA((N_Y + 1,))],
        compiler_params=pltpu.CompilerParams(vmem_limit_bytes=8 * MIB),
        name="norm",
    )(*raw, dec, squares, gain.reshape(D // HD, HD))
    return (decoded.reshape(STEPS, 1, FEAT), scored.reshape(1, PBLK, D))


def solution(mesh):
    placed = (
        P("grp", None, "ulys"),
        P(None, "grp", "ulys"),
        P("ulys", None),
        P(),
        P("grp"),
        P("grp"),
        P(),
    )
    return jax.shard_map(
        body,
        mesh=mesh,
        in_specs=placed,
        out_specs=(P(None, "grp", "ulys"), P("grp", "ulys", None)),
        check_vma=False,
    )
```

```python
import math

import jax
import jax.numpy as jnp
from jax import lax
from jax.experimental import pallas as pl
from jax.experimental.pallas import tpu as pltpu
from jax.sharding import PartitionSpec as P

HD = 128
QPK = 5
GW = 896
FEAT = QPK * HD
CACHE = 512
D = 5120
STEPS = 3
N_GRP = 32
N_ULYS = 8
N_Z = 8
N_Y = 4
PBLK = CACHE // N_ULYS
TILE = PBLK // N_Y
QBLK = 128
N_B = CACHE // QBLK
B_TILES = QBLK // TILE
PAD = 8
WCHUNK = 1280
N_W = D // WCHUNK
EXP2_SCALE = HD ** (-0.5) * math.log2(math.e)
NEG = -1e30
MIB = 1024 * 1024
MESH = pl.DeviceIdType.MESH
CHUNKS = (2, 3)


FIRST = tuple(sum(CHUNKS[:c]) for c in range(len(CHUNKS)))
N_C = len(CHUNKS)
ORDER = (0, 1, 4, 2, 5, 8, 3, 6, 9, 7, 10, 11, 12, 13, 14, 15, 28, 29, 30, 31, 24, 25, 26, 27, 16, 17, 18, 19, 20, 21, 22)
ORDER_LAST = 23


def div(a, n):
    return lax.div(a, jnp.int32(n))


def rem(a, n):
    return lax.rem(a, jnp.int32(n))


def relay_of(head, b, i):
    p = 2 * b + div(i, N_Y)
    return rem(head + p, N_Z) * N_Y + rem(b + i, N_Y), p


def tile_of(z, y, u):
    b = u // 2
    r = (y - b + N_Y) % N_Y
    return (z - u + N_Z) % N_Z, b, (u % 2) * N_Y + r


def attend_block(x, out, b, first, count, limit):
    rows = lax.broadcasted_iota(jnp.int32, (QBLK, 1), 0)
    cols = lax.broadcasted_iota(jnp.int32, (1, QBLK), 1)
    top = b * QBLK
    span = top + QBLK
    keys = x[0:span, FEAT:FEAT + HD]
    values = x[0:span, FEAT + HD:FEAT + 2 * HD]
    live = rows + top < limit
    for j in range(count):
        q = first + j
        query = x[top:span, q * HD:(q + 1) * HD]
        s = lax.dot_general(query, keys, (((1,), (1,)), ((), ())), preferred_element_type=jnp.float32)
        diag = jnp.where(cols <= rows, s[:, top:span], NEG)
        s = diag if b == 0 else jnp.concatenate([s[:, :top], diag], axis=1)
        m = jnp.max(s, axis=1, keepdims=True)
        p = jnp.exp2((s - m) * EXP2_SCALE)
        total = jnp.sum(p, axis=1, keepdims=True)
        o = jnp.dot(p.astype(jnp.bfloat16), values, preferred_element_type=jnp.float32)
        o = jnp.where(live, o * (1.0 / total), 0.0)
        out[top:span, j * HD:(j + 1) * HD] = o.astype(jnp.bfloat16)


def decode_heads(x, fresh, dhead, length):
    keys = x[:, FEAT:FEAT + HD]
    values = x[:, FEAT + HD:FEAT + 2 * HD]
    new_keys = fresh[:, FEAT:FEAT + HD].astype(jnp.bfloat16)
    new_values = fresh[:, FEAT + HD:FEAT + 2 * HD].astype(jnp.bfloat16)
    old_mask = lax.broadcasted_iota(jnp.int32, (1, CACHE), 1) < length
    step = lax.broadcasted_iota(jnp.int32, (PAD, PAD), 0)
    new_mask = lax.broadcasted_iota(jnp.int32, (PAD, PAD), 1) <= step
    dims = (((1,), (1,)), ((), ()))
    for q in range(QPK):
        query = fresh[:, q * HD:(q + 1) * HD].astype(jnp.bfloat16)
        old = lax.dot_general(query, keys, dims, preferred_element_type=jnp.float32)
        new = lax.dot_general(query, new_keys, dims, preferred_element_type=jnp.float32)
        old = jnp.where(old_mask, old, NEG)
        new = jnp.where(new_mask, new, NEG)
        m = jnp.maximum(jnp.max(old, axis=1, keepdims=True), jnp.max(new, axis=1, keepdims=True))
        p_old = jnp.exp2((old - m) * EXP2_SCALE)
        p_new = jnp.exp2((new - m) * EXP2_SCALE)
        total = jnp.sum(p_old, axis=1, keepdims=True) + jnp.sum(p_new, axis=1, keepdims=True)
        o = jnp.dot(p_old.astype(jnp.bfloat16), values, preferred_element_type=jnp.float32)
        o = o + jnp.dot(p_new.astype(jnp.bfloat16), new_values, preferred_element_type=jnp.float32)
        dhead[:, q * HD:(q + 1) * HD] = (o * (1.0 / total)).astype(jnp.bfloat16)


def step_kernel(x_hbm, new_hbm, w_hbm, length_s, done_s, assign_hbm, dec, *buffers):
    raw, scratch = buffers[:N_C], buffers[N_C:]
    heads, recv, stage = scratch[:N_C], scratch[N_C:2 * N_C], scratch[2 * N_C:3 * N_C]
    (x, new, w, assign, found, source, fresh, dhead, part, dec_in,
     x_sem, w_sem, small_sem, send1, recv1, send2, recv2, send3, recv3) = scratch[3 * N_C:]
    me = lax.axis_index("grp")
    u = lax.axis_index("ulys")
    z = me // N_Y
    y = me % N_Y
    g_in, _, i_in = tile_of(z, y, u)
    r_out = i_in % N_Y
    hit1 = jnp.where(g_in == u, 1, 0)

    small = [
        pltpu.make_async_copy(src, dst, small_sem.at[k])
        for k, (src, dst) in enumerate(
            ((assign_hbm, assign), (new_hbm, new)))
    ]
    x_copies = [
        pltpu.make_async_copy(x_hbm.at[0, pl.ds(b * QBLK, QBLK)], x.at[pl.ds(b * QBLK, QBLK)], x_sem.at[b])
        for b in range(N_B)
    ]
    w_copies = [
        pltpu.make_async_copy(w_hbm.at[:, pl.ds(c * WCHUNK, WCHUNK)], w.at[c], w_sem.at[c]) for c in range(N_W)
    ]
    for copy in x_copies:
        copy.start()

    barrier = pltpu.get_barrier_semaphore()

    def greet(grp, ulys):
        pl.semaphore_signal(barrier, inc=1, device_id=(grp, ulys), device_id_type=MESH)

    @pl.loop(1, N_GRP, unroll=True)
    def _(k):
        greet(rem(me + k, N_GRP), g_in)

    @pl.loop(1, N_ULYS, unroll=True)
    def _(k):
        greet(me, rem(u + k, N_ULYS))

    @pl.when(g_in != u)
    def _():
        greet(me, g_in)

    for copy in small:
        copy.start()

    length = length_s[0]
    done = done_s[0]
    limit = length * done

    for c in range(N_C):
        for b in range(N_B):
            if c == 0:
                x_copies[b].wait()
            attend_block(x, heads[c], b, FIRST[c], CHUNKS[c], limit)
        if c == 0:
            pl.semaphore_wait(barrier, N_GRP - hit1 + N_ULYS - 1)

        @pl.loop(0, N_GRP)
        def _(k, c=c):
            b = rem(div(k, B_TILES) + z + y, N_B)
            i = rem(k + y + z, B_TILES)
            grp, ulys = relay_of(u, b, i)
            src = heads[c].at[pl.ds(pl.multiple_of(b * QBLK + i * TILE, TILE), TILE)]
            own = (grp == me) & (ulys == u)

            @pl.when(own)
            def _():
                pltpu.make_async_copy(src, recv[c].at[me], recv1.at[c]).start()

            @pl.when(jnp.logical_not(own))
            def _():
                pltpu.make_async_remote_copy(
                    src, recv[c].at[me], send1.at[c], recv1.at[c], device_id=(grp, ulys), device_id_type=MESH
                ).start()

    for copy in w_copies:
        copy.start()
    small[0].wait()
    place = lax.broadcasted_iota(jnp.int32, (N_GRP, HD), 0)
    group = jnp.zeros((N_GRP, HD), jnp.int32)
    for n in range(N_GRP):
        group = jnp.where(place == n, assign[n], group)
    lanes = lax.broadcasted_iota(jnp.int32, (N_GRP, HD), 1)
    found[...] = jnp.max(jnp.where(group == lanes, place, 0), axis=0, keepdims=True)
    to_scalars = pltpu.make_async_copy(found, source, small_sem.at[0])
    to_scalars.start()
    to_scalars.wait()

    slot = g_in * N_Y + r_out
    for c in range(N_C):
        pltpu.make_async_copy(recv[c], recv[c], recv1.at[c]).wait()

        def forward(t, c=c):
            stage[c][t] = recv[c][source[0, t]]
            pltpu.make_async_remote_copy(
                stage[c].at[t], raw[c].at[slot], send2.at[c], recv2.at[c], device_id=(t, u), device_id_type=MESH
            ).start()

        if c + 1 < N_C:
            @pl.loop(0, N_GRP - 1)
            def _(k):
                t = rem(k, N_Z) * N_Y + div(k, N_Z)
                forward(jnp.where(t == me, N_GRP - 1, t))
        else:
            for t in ORDER:
                forward(jnp.where(me == t, ORDER_LAST, t))

        stage[c][me] = recv[c][source[0, me]]
        pltpu.make_async_copy(stage[c].at[me], raw[c].at[slot], recv2.at[c]).start()

        if c > 0:
            continue
        small[1].wait()
        fresh[...] = jnp.zeros_like(fresh)
        fresh[0:STEPS, :] = new[...].astype(jnp.float32)
        decode_heads(x, fresh, dhead, length)
        lhs = dhead[...]
        for k in range(N_W):
            w_copies[k].wait()
            part[:, k * WCHUNK:(k + 1) * WCHUNK] = jnp.dot(lhs, w[k], preferred_element_type=jnp.float32)

        @pl.loop(1, N_ULYS)
        def _(k):
            p = rem(u + k, N_ULYS)
            pltpu.make_async_remote_copy(
                part.at[:, pl.ds(pl.multiple_of(p * FEAT, HD), FEAT)],
                dec_in.at[u], send3, recv3, device_id=(me, p), device_id_type=MESH
            ).start()

        pltpu.make_async_copy(part.at[:, pl.ds(pl.multiple_of(u * FEAT, HD), FEAT)], dec_in.at[u], recv3).start()

    pltpu.make_async_copy(dec_in, dec_in, recv3).wait()
    total = dec_in[0]
    for g in range(1, N_ULYS):
        total = total + dec_in[g]
    dec[...] = (total * (1 - done).astype(jnp.float32))[0:STEPS].astype(jnp.bfloat16)

    for c in range(N_C):
        pltpu.make_async_copy(recv[c], recv[c], recv2.at[c]).wait()
    for c in range(N_C):
        sent = stage[c].at[pl.ds(0, N_GRP - 1)]
        pltpu.make_async_copy(sent, sent, send2.at[c]).wait()

        @pl.when(hit1 > 0)
        def _(c=c, sent=sent):
            pltpu.make_async_copy(sent, sent, send1.at[c]).wait()

        @pl.when(hit1 <= 0)
        def _(c=c):
            pltpu.make_async_copy(stage[c], stage[c], send1.at[c]).wait()

    sent = dec_in.at[pl.ds(0, N_ULYS - 1)]
    pltpu.make_async_copy(sent, sent, send3).wait()


def norm_kernel(*refs):
    raw = refs[:N_C]
    dec, gain, decoded, scored, out, sem = refs[N_C:]
    copies = [pltpu.make_async_copy(dec, decoded, sem.at[N_Y])]
    copies[0].start()
    gains = gain[...].astype(jnp.float32)
    places = [(g, c, j) for g in range(N_ULYS) for c in range(N_C) for j in range(CHUNKS[c])]
    for r in range(N_Y):
        rows = slice(r * TILE, (r + 1) * TILE)
        square = jnp.zeros((TILE, HD), jnp.float32)
        for g, c, j in places:
            lifted = raw[c][g * N_Y + r, :, j * HD:(j + 1) * HD].astype(jnp.float32)
            square = square + lifted * lifted
        power = jnp.sum(square, axis=1, keepdims=True) * (1.0 / D)
        factor = lax.rsqrt(power + 1e-06)
        for k, (g, c, j) in enumerate(places):
            lifted = raw[c][g * N_Y + r, :, j * HD:(j + 1) * HD].astype(jnp.float32)
            out[rows, k * HD:(k + 1) * HD] = (lifted * factor * gains[k:k + 1]).astype(jnp.bfloat16)
        at = pl.ds(r * TILE, TILE)
        copies.append(pltpu.make_async_copy(out.at[at], scored.at[at], sem.at[r]))
        copies[-1].start()
    for copy in copies:
        copy.wait()


def body(layer_states, new_states, out_proj, gain, lengths, finished, assignment):
    hbm = pl.BlockSpec(memory_space=pl.ANY)
    vmem = pl.BlockSpec(memory_space=pltpu.VMEM)
    smem = pl.BlockSpec(memory_space=pltpu.SMEM)

    def pinned(a):
        return pltpu.with_memory_space_constraint(a, pltpu.HBM)

    dec, *raw = pl.pallas_call(
        step_kernel,
        out_shape=(
            pltpu.VMEM((STEPS, FEAT), jnp.bfloat16),
        ) + tuple(pltpu.VMEM((N_GRP, TILE, n * HD), jnp.bfloat16) for n in CHUNKS),
        in_specs=[hbm] * 3 + [smem] * 2 + [hbm],
        out_specs=(vmem,) * (1 + N_C),
        scratch_shapes=[pltpu.VMEM((CACHE, n * HD), jnp.bfloat16) for n in CHUNKS]
        + [pltpu.VMEM((N_GRP, TILE, n * HD), jnp.bfloat16) for n in CHUNKS] * 2
        + [
            pltpu.VMEM((CACHE, GW), jnp.bfloat16),
            pltpu.VMEM((STEPS, GW), jnp.bfloat16),
            pltpu.VMEM((N_W, FEAT, WCHUNK), jnp.bfloat16),
            pltpu.SMEM((N_GRP,), jnp.int32),
            pltpu.VMEM((1, HD), jnp.int32),
            pltpu.SMEM((1, HD), jnp.int32),
            pltpu.VMEM((PAD, GW), jnp.float32),
            pltpu.VMEM((PAD, FEAT), jnp.bfloat16),
            pltpu.VMEM((PAD, D), jnp.float32),
            pltpu.VMEM((N_ULYS, PAD, FEAT), jnp.float32),
            pltpu.SemaphoreType.DMA((N_B,)),
            pltpu.SemaphoreType.DMA((N_W,)),
            pltpu.SemaphoreType.DMA((2,)),
        ]
        + [pltpu.SemaphoreType.DMA((N_C,))] * 4
        + [pltpu.SemaphoreType.DMA] * 2,
        compiler_params=pltpu.CompilerParams(
            vmem_limit_bytes=32 * MIB, collective_id=0, has_side_effects=True
        ),
        name="step",
    )(
        pinned(layer_states), pinned(new_states.reshape(STEPS, GW)), pinned(out_proj),
        lengths, finished, pinned(assignment),
    )
    decoded, scored = pl.pallas_call(
        norm_kernel,
        out_shape=(
            jax.ShapeDtypeStruct((STEPS, FEAT), jnp.bfloat16),
            jax.ShapeDtypeStruct((PBLK, D), jnp.bfloat16),
        ),
        in_specs=[vmem] * (2 + N_C),
        out_specs=(hbm, hbm),
        scratch_shapes=[pltpu.VMEM((PBLK, D), jnp.bfloat16), pltpu.SemaphoreType.DMA((N_Y + 1,))],
        compiler_params=pltpu.CompilerParams(vmem_limit_bytes=8 * MIB),
        name="norm",
    )(*raw, dec, gain.reshape(D // HD, HD))
    return (decoded.reshape(STEPS, 1, FEAT), scored.reshape(1, PBLK, D))


def solution(mesh):
    placed = (
        P("grp", None, "ulys"),
        P(None, "grp", "ulys"),
        P("ulys", None),
        P(),
        P("grp"),
        P("grp"),
        P(),
    )
    return jax.shard_map(
        body,
        mesh=mesh,
        in_specs=placed,
        out_specs=(P(None, "grp", "ulys"), P("grp", "ulys", None)),
        check_vma=False,
    )
```

```python
import math

import jax
import jax.numpy as jnp
from jax import lax
from jax.experimental import pallas as pl
from jax.experimental.pallas import tpu as pltpu
from jax.sharding import PartitionSpec as P

HD = 128
QPK = 5
GW = 896
FEAT = QPK * HD
CACHE = 512
D = 5120
STEPS = 3
N_GRP = 32
N_ULYS = 8
N_Z = 8
N_Y = 4
PBLK = CACHE // N_ULYS
TILE = PBLK // N_Y
QBLK = 128
N_B = CACHE // QBLK
B_TILES = QBLK // TILE
PAD = 8
WCHUNK = 1280
N_W = D // WCHUNK
EXP2_SCALE = HD ** (-0.5) * math.log2(math.e)
NEG = -1e30
MIB = 1024 * 1024
MESH = pl.DeviceIdType.MESH
CHUNKS = (2, 3)


FIRST = tuple(sum(CHUNKS[:c]) for c in range(len(CHUNKS)))
N_C = len(CHUNKS)
ORDER = (0, 3, 4, 1, 7, 8, 2, 11, 5, 6, 9, 10, 12, 13, 14, 15, 28, 29, 30, 31, 24, 25, 26, 27, 16, 17, 18, 19, 20, 21, 22)
ORDER_LAST = 23


def div(a, n):
    return lax.div(a, jnp.int32(n))


def rem(a, n):
    return lax.rem(a, jnp.int32(n))


def relay_of(head, b, i):
    p = 2 * b + div(i, N_Y)
    return rem(head + p, N_Z) * N_Y + rem(b + i, N_Y), p


def tile_of(z, y, u):
    b = u // 2
    r = (y - b + N_Y) % N_Y
    return (z - u + N_Z) % N_Z, b, (u % 2) * N_Y + r


def attend_block(x, out, b, first, count, limit):
    rows = lax.broadcasted_iota(jnp.int32, (QBLK, 1), 0)
    cols = lax.broadcasted_iota(jnp.int32, (1, QBLK), 1)
    top = b * QBLK
    span = top + QBLK
    keys = x[0:span, FEAT:FEAT + HD]
    values = x[0:span, FEAT + HD:FEAT + 2 * HD]
    live = rows + top < limit
    for j in range(count):
        q = first + j
        query = x[top:span, q * HD:(q + 1) * HD]
        s = lax.dot_general(query, keys, (((1,), (1,)), ((), ())), preferred_element_type=jnp.float32)
        diag = jnp.where(cols <= rows, s[:, top:span], NEG)
        s = diag if b == 0 else jnp.concatenate([s[:, :top], diag], axis=1)
        m = jnp.max(s, axis=1, keepdims=True)
        p = jnp.exp2((s - m) * EXP2_SCALE)
        total = jnp.sum(p, axis=1, keepdims=True)
        o = jnp.dot(p.astype(jnp.bfloat16), values, preferred_element_type=jnp.float32)
        o = jnp.where(live, o * (1.0 / total), 0.0)
        out[top:span, j * HD:(j + 1) * HD] = o.astype(jnp.bfloat16)


def decode_heads(x, fresh, dhead, length):
    keys = x[:, FEAT:FEAT + HD]
    values = x[:, FEAT + HD:FEAT + 2 * HD]
    new_keys = fresh[:, FEAT:FEAT + HD].astype(jnp.bfloat16)
    new_values = fresh[:, FEAT + HD:FEAT + 2 * HD].astype(jnp.bfloat16)
    old_mask = lax.broadcasted_iota(jnp.int32, (1, CACHE), 1) < length
    step = lax.broadcasted_iota(jnp.int32, (PAD, PAD), 0)
    new_mask = lax.broadcasted_iota(jnp.int32, (PAD, PAD), 1) <= step
    dims = (((1,), (1,)), ((), ()))
    for q in range(QPK):
        query = fresh[:, q * HD:(q + 1) * HD].astype(jnp.bfloat16)
        old = lax.dot_general(query, keys, dims, preferred_element_type=jnp.float32)
        new = lax.dot_general(query, new_keys, dims, preferred_element_type=jnp.float32)
        old = jnp.where(old_mask, old, NEG)
        new = jnp.where(new_mask, new, NEG)
        m = jnp.maximum(jnp.max(old, axis=1, keepdims=True), jnp.max(new, axis=1, keepdims=True))
        p_old = jnp.exp2((old - m) * EXP2_SCALE)
        p_new = jnp.exp2((new - m) * EXP2_SCALE)
        total = jnp.sum(p_old, axis=1, keepdims=True) + jnp.sum(p_new, axis=1, keepdims=True)
        o = jnp.dot(p_old.astype(jnp.bfloat16), values, preferred_element_type=jnp.float32)
        o = o + jnp.dot(p_new.astype(jnp.bfloat16), new_values, preferred_element_type=jnp.float32)
        dhead[:, q * HD:(q + 1) * HD] = (o * (1.0 / total)).astype(jnp.bfloat16)


def step_kernel(x_hbm, new_hbm, w_hbm, length_s, done_s, assign_hbm, dec, *buffers):
    raw, scratch = buffers[:N_C], buffers[N_C:]
    heads, recv, stage = scratch[:N_C], scratch[N_C:2 * N_C], scratch[2 * N_C:3 * N_C]
    (x, new, w, assign, found, source, fresh, dhead, part, dec_in,
     x_sem, w_sem, small_sem, send1, recv1, send2, recv2, send3, recv3) = scratch[3 * N_C:]
    me = lax.axis_index("grp")
    u = lax.axis_index("ulys")
    z = me // N_Y
    y = me % N_Y
    g_in, _, i_in = tile_of(z, y, u)
    r_out = i_in % N_Y
    hit1 = jnp.where(g_in == u, 1, 0)

    small = [
        pltpu.make_async_copy(src, dst, small_sem.at[k])
        for k, (src, dst) in enumerate(
            ((assign_hbm, assign), (new_hbm, new)))
    ]
    x_copies = [
        pltpu.make_async_copy(x_hbm.at[0, pl.ds(b * QBLK, QBLK)], x.at[pl.ds(b * QBLK, QBLK)], x_sem.at[b])
        for b in range(N_B)
    ]
    w_copies = [
        pltpu.make_async_copy(w_hbm.at[:, pl.ds(c * WCHUNK, WCHUNK)], w.at[c], w_sem.at[c]) for c in range(N_W)
    ]
    for copy in x_copies:
        copy.start()

    barrier = pltpu.get_barrier_semaphore()

    def greet(grp, ulys):
        pl.semaphore_signal(barrier, inc=1, device_id=(grp, ulys), device_id_type=MESH)

    @pl.loop(1, N_GRP, unroll=True)
    def _(k):
        greet(rem(me + k, N_GRP), g_in)

    @pl.loop(1, N_ULYS, unroll=True)
    def _(k):
        greet(me, rem(u + k, N_ULYS))

    @pl.when(g_in != u)
    def _():
        greet(me, g_in)

    for copy in small:
        copy.start()

    length = length_s[0]
    done = done_s[0]
    limit = length * done

    for c in range(N_C):
        for b in range(N_B):
            if c == 0:
                x_copies[b].wait()
            attend_block(x, heads[c], b, FIRST[c], CHUNKS[c], limit)
        if c == 0:
            pl.semaphore_wait(barrier, N_GRP - hit1 + N_ULYS - 1)

        @pl.loop(0, N_GRP)
        def _(k, c=c):
            b = rem(div(k, B_TILES) + z + y, N_B)
            i = rem(k + y + z, B_TILES)
            grp, ulys = relay_of(u, b, i)
            src = heads[c].at[pl.ds(pl.multiple_of(b * QBLK + i * TILE, TILE), TILE)]
            own = (grp == me) & (ulys == u)

            @pl.when(own)
            def _():
                pltpu.make_async_copy(src, recv[c].at[me], recv1.at[c]).start()

            @pl.when(jnp.logical_not(own))
            def _():
                pltpu.make_async_remote_copy(
                    src, recv[c].at[me], send1.at[c], recv1.at[c], device_id=(grp, ulys), device_id_type=MESH
                ).start()

    for copy in w_copies:
        copy.start()
    small[0].wait()
    place = lax.broadcasted_iota(jnp.int32, (N_GRP, HD), 0)
    group = jnp.zeros((N_GRP, HD), jnp.int32)
    for n in range(N_GRP):
        group = jnp.where(place == n, assign[n], group)
    lanes = lax.broadcasted_iota(jnp.int32, (N_GRP, HD), 1)
    found[...] = jnp.max(jnp.where(group == lanes, place, 0), axis=0, keepdims=True)
    to_scalars = pltpu.make_async_copy(found, source, small_sem.at[0])
    to_scalars.start()
    to_scalars.wait()

    slot = g_in * N_Y + r_out
    for c in range(N_C):
        pltpu.make_async_copy(recv[c], recv[c], recv1.at[c]).wait()

        def forward(t, c=c):
            stage[c][t] = recv[c][source[0, t]]
            pltpu.make_async_remote_copy(
                stage[c].at[t], raw[c].at[slot], send2.at[c], recv2.at[c], device_id=(t, u), device_id_type=MESH
            ).start()

        if c + 1 < N_C:
            @pl.loop(0, N_GRP - 1)
            def _(k):
                t = rem(k, N_Z) * N_Y + div(k, N_Z)
                forward(jnp.where(t == me, N_GRP - 1, t))
        else:
            for t in ORDER:
                forward(jnp.where(me == t, ORDER_LAST, t))

        stage[c][me] = recv[c][source[0, me]]
        pltpu.make_async_copy(stage[c].at[me], raw[c].at[slot], recv2.at[c]).start()

        if c > 0:
            continue
        small[1].wait()
        fresh[...] = jnp.zeros_like(fresh)
        fresh[0:STEPS, :] = new[...].astype(jnp.float32)
        decode_heads(x, fresh, dhead, length)
        lhs = dhead[...]
        for k in range(N_W):
            w_copies[k].wait()
            part[:, k * WCHUNK:(k + 1) * WCHUNK] = jnp.dot(lhs, w[k], preferred_element_type=jnp.float32)

        @pl.loop(1, N_ULYS)
        def _(k):
            p = rem(u + k, N_ULYS)
            pltpu.make_async_remote_copy(
                part.at[:, pl.ds(pl.multiple_of(p * FEAT, HD), FEAT)],
                dec_in.at[u], send3, recv3, device_id=(me, p), device_id_type=MESH
            ).start()

        pltpu.make_async_copy(part.at[:, pl.ds(pl.multiple_of(u * FEAT, HD), FEAT)], dec_in.at[u], recv3).start()

    pltpu.make_async_copy(dec_in, dec_in, recv3).wait()
    total = dec_in[0]
    for g in range(1, N_ULYS):
        total = total + dec_in[g]
    dec[...] = (total * (1 - done).astype(jnp.float32))[0:STEPS].astype(jnp.bfloat16)

    for c in range(N_C):
        pltpu.make_async_copy(recv[c], recv[c], recv2.at[c]).wait()
    for c in range(N_C):
        sent = stage[c].at[pl.ds(0, N_GRP - 1)]
        pltpu.make_async_copy(sent, sent, send2.at[c]).wait()

        @pl.when(hit1 > 0)
        def _(c=c, sent=sent):
            pltpu.make_async_copy(sent, sent, send1.at[c]).wait()

        @pl.when(hit1 <= 0)
        def _(c=c):
            pltpu.make_async_copy(stage[c], stage[c], send1.at[c]).wait()

    sent = dec_in.at[pl.ds(0, N_ULYS - 1)]
    pltpu.make_async_copy(sent, sent, send3).wait()


def norm_kernel(*refs):
    raw = refs[:N_C]
    dec, gain, decoded, scored, out, sem = refs[N_C:]
    copies = [pltpu.make_async_copy(dec, decoded, sem.at[N_Y])]
    copies[0].start()
    gains = gain[...].astype(jnp.float32)
    places = [(g, c, j) for g in range(N_ULYS) for c in range(N_C) for j in range(CHUNKS[c])]
    for r in range(N_Y):
        rows = slice(r * TILE, (r + 1) * TILE)
        square = jnp.zeros((TILE, HD), jnp.float32)
        for g, c, j in places:
            lifted = raw[c][g * N_Y + r, :, j * HD:(j + 1) * HD].astype(jnp.float32)
            square = square + lifted * lifted
        power = jnp.sum(square, axis=1, keepdims=True) * (1.0 / D)
        factor = lax.rsqrt(power + 1e-06)
        for k, (g, c, j) in enumerate(places):
            lifted = raw[c][g * N_Y + r, :, j * HD:(j + 1) * HD].astype(jnp.float32)
            out[rows, k * HD:(k + 1) * HD] = (lifted * factor * gains[k:k + 1]).astype(jnp.bfloat16)
        at = pl.ds(r * TILE, TILE)
        copies.append(pltpu.make_async_copy(out.at[at], scored.at[at], sem.at[r]))
        copies[-1].start()
    for copy in copies:
        copy.wait()


def body(layer_states, new_states, out_proj, gain, lengths, finished, assignment):
    hbm = pl.BlockSpec(memory_space=pl.ANY)
    vmem = pl.BlockSpec(memory_space=pltpu.VMEM)
    smem = pl.BlockSpec(memory_space=pltpu.SMEM)

    def pinned(a):
        return pltpu.with_memory_space_constraint(a, pltpu.HBM)

    dec, *raw = pl.pallas_call(
        step_kernel,
        out_shape=(
            pltpu.VMEM((STEPS, FEAT), jnp.bfloat16),
        ) + tuple(pltpu.VMEM((N_GRP, TILE, n * HD), jnp.bfloat16) for n in CHUNKS),
        in_specs=[hbm] * 3 + [smem] * 2 + [hbm],
        out_specs=(vmem,) * (1 + N_C),
        scratch_shapes=[pltpu.VMEM((CACHE, n * HD), jnp.bfloat16) for n in CHUNKS]
        + [pltpu.VMEM((N_GRP, TILE, n * HD), jnp.bfloat16) for n in CHUNKS] * 2
        + [
            pltpu.VMEM((CACHE, GW), jnp.bfloat16),
            pltpu.VMEM((STEPS, GW), jnp.bfloat16),
            pltpu.VMEM((N_W, FEAT, WCHUNK), jnp.bfloat16),
            pltpu.SMEM((N_GRP,), jnp.int32),
            pltpu.VMEM((1, HD), jnp.int32),
            pltpu.SMEM((1, HD), jnp.int32),
            pltpu.VMEM((PAD, GW), jnp.float32),
            pltpu.VMEM((PAD, FEAT), jnp.bfloat16),
            pltpu.VMEM((PAD, D), jnp.float32),
            pltpu.VMEM((N_ULYS, PAD, FEAT), jnp.float32),
            pltpu.SemaphoreType.DMA((N_B,)),
            pltpu.SemaphoreType.DMA((N_W,)),
            pltpu.SemaphoreType.DMA((2,)),
        ]
        + [pltpu.SemaphoreType.DMA((N_C,))] * 4
        + [pltpu.SemaphoreType.DMA] * 2,
        compiler_params=pltpu.CompilerParams(
            vmem_limit_bytes=32 * MIB, collective_id=0, has_side_effects=True
        ),
        name="step",
    )(
        pinned(layer_states), pinned(new_states.reshape(STEPS, GW)), pinned(out_proj),
        lengths, finished, pinned(assignment),
    )
    decoded, scored = pl.pallas_call(
        norm_kernel,
        out_shape=(
            jax.ShapeDtypeStruct((STEPS, FEAT), jnp.bfloat16),
            jax.ShapeDtypeStruct((PBLK, D), jnp.bfloat16),
        ),
        in_specs=[vmem] * (2 + N_C),
        out_specs=(hbm, hbm),
        scratch_shapes=[pltpu.VMEM((PBLK, D), jnp.bfloat16), pltpu.SemaphoreType.DMA((N_Y + 1,))],
        compiler_params=pltpu.CompilerParams(vmem_limit_bytes=8 * MIB),
        name="norm",
    )(*raw, dec, gain.reshape(D // HD, HD))
    return (decoded.reshape(STEPS, 1, FEAT), scored.reshape(1, PBLK, D))


def solution(mesh):
    placed = (
        P("grp", None, "ulys"),
        P(None, "grp", "ulys"),
        P("ulys", None),
        P(),
        P("grp"),
        P("grp"),
        P(),
    )
    return jax.shard_map(
        body,
        mesh=mesh,
        in_specs=placed,
        out_specs=(P(None, "grp", "ulys"), P("grp", "ulys", None)),
        check_vma=False,
    )
```
